256 devices in a mesh: dp: 8 (over z), expert: 32 (over y, x, core).
Axes of the slice: x: 4, y: 4, z: 8, core: 2. Of those that a mesh axis runs over, the one named last changes fastest.
Arguments:
- hidden_in: bfloat16 [32768, 1024], P(('dp', 'expert')), may hold values from -6 to 6
- rank_grad: bfloat16 [32768, 1024], P(('dp', 'expert')), may hold values from -6 to 6
- gates: bfloat16 [32768, 8], P(('dp', 'expert')), may hold values from 0.049804688 to 1
- expert_ids: int32 [32768, 8], P(('dp', 'expert')), may hold values from 0 to 63, all different within a row; in each aligned block of 128 rows (0 to 127, 128 to 255, ...) at most 32 rows name the same one
- cores: bfloat16 [64, 1024, 1024], P('expert'), may hold values from -0.1875 to 0.1875
Outputs:
- rank_input_grad: bfloat16 [32768, 1024], P(('dp', 'expert'))
- core_grad: float32 [1024, 64, 1024], P('dp', 'expert')
The draws below stay inside these ranges and needn't reach their ends.
Inputs may be any that keep to these rules, and one draw needn't show every extreme that they name: `expert_ids`: each row names 8 different experts; among the rows of one device no expert is named more than 32 times, a bound that some block reaches.
All inputs are finite; a program needn't handle non-finite values.
Results may differ from the reference program's by a relative error of at most 0.0057.
Values may be sent and summed in bfloat16 or wider, within the bound.
A program may use at most 128 MiB of HBM per device.

```python
import math
import jax
import jax.numpy as jnp
import numpy as np
from jax import lax

R = 1024
TOPK = 8
TOK_DEV = 128
EXPERTS = 64
CAP = 32
TOKENS = 32768


def block_scale(own_key, dims, cuts, least, largest):
    level, own = 1.0, jax.random.fold_in(own_key, 6)
    for position, parts in cuts:
        heights = jnp.exp(jax.random.uniform(jax.random.fold_in(own, position), (parts,), jnp.float32, least / len(cuts), largest / len(cuts)))
        level = level * jnp.repeat(heights, dims[position] // parts).reshape([-1 if axis == position else 1 for axis in range(len(dims))])
    return level


def assign_block(stream_key, own, number, rows, number_of, top, reach, skew):
    order = jax.random.permutation(stream_key, number_of)
    heavy_load, ordinary = load_shares(number_of, rows * top, reach, skew, True), load_shares(number_of, rows * top, reach, skew, False)
    places = jnp.arange(number_of)

    def named(tallies, rotation):
        used = int((tallies > 0).sum())
        fixed = max(1, used // 4)
        shifted = fixed + (places - fixed + rotation * (used - fixed)) % max(1, number_of - fixed)
        return jnp.zeros((number_of,), jnp.int32).at[order[jnp.where(places < fixed, places, shifted)]].set(jnp.asarray(tallies, jnp.int32))

    tallies = jnp.where(number % 4 == 0, named(heavy_load, number // 4), named(ordinary, number - number // 4 - 1))
    mixed = jax.random.permutation(jax.random.fold_in(own, 3), number_of)
    giver, sink = mixed[0:number_of // 2 * 2:2], mixed[1:number_of // 2 * 2:2]
    margin = jnp.minimum(tallies[giver] - 1, reach - tallies[sink]) // 2
    margin = jnp.where((giver == order[0]) | (sink == order[0]) | (tallies[sink] == 0), 0, jnp.maximum(margin, 0))
    shifted = jax.random.randint(jax.random.fold_in(own, 4), (number_of // 2,), 0, 1 << 20) % (margin + 1)
    tallies = tallies.at[giver].add(-shifted).at[sink].add(shifted)
    labels = jnp.searchsorted(jnp.cumsum(tallies), jnp.arange(rows * top), side="right").astype(jnp.int32)
    table = labels.reshape(top, rows).T
    table = table[jax.random.permutation(jax.random.fold_in(own, 1), rows)]
    rotation = jax.random.randint(jax.random.fold_in(own, 2), (rows, 1), 0, top)
    return jnp.take_along_axis(table, (jnp.arange(top)[None, :] + rotation) % top, axis=1)


def load_shares(amount, total, most, skew, full):
    portions = [(1 << 20) // math.isqrt(grade ** skew) + 1 for grade in range(1, amount + 1)]
    largest = most if full else min(most, max(-(-total // amount), total * portions[0] // sum(portions)))
    least = 1 if total - largest >= amount - 1 else 0
    given, spare = [largest] + [least] * (amount - 1), total - largest - least * (amount - 1)
    while spare > 0:
        candidates = [i for i in range(1, amount) if given[i] < largest] or [i for i in range(1, amount) if given[i] < most]
        pool, budget = sum([portions[i] for i in candidates]), spare
        for i in candidates:
            extra = min(most - given[i], max(1, budget * portions[i] // pool), spare)
            given[i] = given[i] + extra
            spare = spare - extra
    return np.array(given)


def bell_draw(rng, extent, scale, limit, shards=(), kind=jnp.bfloat16):
    level = block_scale(rng, extent, shards, -0.22, 0.18) if shards else 1.0
    values = jax.random.normal(rng, extent, jnp.float32) * scale * level
    return jnp.minimum(jnp.maximum(values, -limit), limit).astype(kind)


def setup_inputs(seed: int = 0) -> dict:
    streams_of = jax.random.split(jax.random.key(seed), 6)
    hidden_in = bell_draw(streams_of[0], (TOKENS, R), 1.0, 6.0, ((0, 256),))
    rank_grad = bell_draw(streams_of[1], (TOKENS, R), 1.0, 6.0, ((0, 256),))
    gates = jnp.clip(jnp.exp(math.log(1.0) - 2.9996462 * jax.random.uniform(streams_of[2], (TOKENS, TOPK), jnp.float32) ** block_scale(streams_of[2], (TOKENS, TOPK), ((0, 256),), -0.2, 0.2)), 0.049804688, 1.0).astype(jnp.bfloat16)
    expert_ids_keys = jax.random.split(jax.random.fold_in(streams_of[3], 1), TOKENS // TOK_DEV)
    expert_ids_turns = jax.random.permutation(jax.random.fold_in(streams_of[3], 3), TOKENS // TOK_DEV)
    expert_ids = jax.vmap(lambda own, number: assign_block(jax.random.fold_in(streams_of[3], 2), own, number, TOK_DEV, EXPERTS, TOPK, CAP, 2))(expert_ids_keys, expert_ids_turns).reshape((TOKENS, TOPK))
    cores = bell_draw(streams_of[4], (EXPERTS, R, R), R ** -0.5, 0.1875, ((0, 32),))
    return {"hidden_in": hidden_in, "rank_grad": rank_grad, "gates": gates, "expert_ids": expert_ids, "cores": cores}


def reference(hidden_in, rank_grad, gates, expert_ids, cores):
    block_rows = 512
    pair_total = TOKENS * TOPK
    chosen = expert_ids.reshape(-1).astype(jnp.int32)
    sorted_pairs = jnp.argsort(chosen, stable=True).astype(jnp.int32)
    counts = jnp.bincount(chosen, length=EXPERTS).astype(jnp.int32)
    begins = (jnp.cumsum(counts) - counts).astype(jnp.int32)
    padded = ((counts + block_rows - 1) // block_rows * block_rows).astype(jnp.int32)
    padded_begins = (jnp.cumsum(padded) - padded).astype(jnp.int32)
    sorted_experts = chosen[sorted_pairs]
    within = jnp.arange(pair_total, dtype=jnp.int32) - begins[sorted_experts]
    targets = (padded_begins[sorted_experts] + within).astype(jnp.int32)
    padded_total = pair_total + EXPERTS * block_rows
    block_count = padded_total // block_rows
    owners = jnp.full((padded_total,), -1, jnp.int32).at[targets].set(sorted_pairs)
    block_firsts = jnp.arange(block_count, dtype=jnp.int32) * block_rows
    padded_ends = padded_begins + padded
    block_experts = jnp.sum((padded_ends[None, :] <= block_firsts[:, None]).astype(jnp.int32), axis=1)
    block_experts = jnp.minimum(block_experts, EXPERTS - 1).astype(jnp.int32)
    gate_flat = gates.reshape(-1)

    def block_step(gradient, carried):
        owned, expert_now = carried
        filled = owned >= 0
        picks = jnp.maximum(owned, 0)
        rows_z = jnp.where(filled[:, None], hidden_in[picks // TOPK], jnp.zeros((), jnp.bfloat16))
        rows_r = jnp.where(filled[:, None], rank_grad[picks // TOPK], jnp.zeros((), jnp.bfloat16))
        rows_g = jnp.where(filled, gate_flat[picks], jnp.zeros((), jnp.bfloat16))
        core_block = cores[expert_now]
        upper = jnp.dot(rows_z, core_block, preferred_element_type=jnp.float32)
        sig = jax.nn.sigmoid(upper)
        slope = sig * (1.0 + upper * (1.0 - sig))
        lowered = (rows_r.astype(jnp.float32) * rows_g.astype(jnp.float32)[:, None] * slope).astype(jnp.bfloat16)
        back = jnp.dot(lowered, core_block.T, preferred_element_type=jnp.float32).astype(jnp.bfloat16)
        term = jnp.dot(rows_z.T, lowered, preferred_element_type=jnp.float32)
        gradient = gradient.at[expert_now].add(term)
        return gradient, back

    gradient, backs = lax.scan(block_step, jnp.zeros((EXPERTS, R, R), jnp.float32),
                               (owners.reshape(block_count, block_rows), block_experts))
    backs = backs.reshape(padded_total, R)
    pair_place = jnp.zeros((pair_total,), jnp.int32).at[sorted_pairs].set(targets).reshape(TOKENS, TOPK)
    total = jnp.zeros((TOKENS, R), jnp.float32)
    for choice_k in range(TOPK):
        total = total + backs[pair_place[:, choice_k]].astype(jnp.float32)
    return total.astype(jnp.bfloat16), jnp.transpose(gradient, (1, 0, 2))
```

```python
import jax
import jax.numpy as jnp
from jax import lax
from jax.experimental import pallas as pl
from jax.experimental.pallas import tpu as pltpu
from jax.sharding import PartitionSpec as P

MESH = pl.DeviceIdType.MESH
F32 = jnp.float32
BF16 = jnp.bfloat16
NZ, NY, NX = 8, 4, 4
CQ = 256
NQ = 4
TOK = 128
CAP = 32
NS = NY * NX
ROWS = NS * CAP


def when(cond, fn):
    if isinstance(cond, bool):
        if cond:
            fn()
    else:
        pl.when(cond)(fn)


def cols(i):
    if isinstance(i, int):
        return pl.ds(i * CQ, CQ)
    return pl.ds(pl.multiple_of(i * CQ, CQ), CQ)


def body(
    h_ref, r_ref, meta_ref, cores_ref,
    rig_ref, cg_ref,
    ag, mb, core, zc, st, gs, lw, zct, bk, sel, selt, gc, asg, code, gts,
    z1, zs1, z2p, z2, z3, z4, rs1, rs2, rs3, rs4,
    core_sem, ag_s, ag_r, mt_s, mt_r, d2_s, d2_r, z_s, z_r, rs_s, rs_r,
):
    z = lax.axis_index("dp")
    ei = lax.axis_index("expert")
    c = lax.rem(ei, 2)
    x = lax.rem(lax.div(ei, 2), NX)
    y = lax.div(ei, 2 * NX)

    def wx(v):
        return lax.rem(v + NX, NX)

    def wz(v):
        return lax.rem(v + NZ, NZ)

    def dev(zz, yy, xx, cc):
        return (zz, (yy * NX + xx) * 2 + cc)

    def to_x(s):
        return dev(z, y, wx(x + s), c)

    def to_y(s):
        return dev(z, wx(y + s), x, c)

    def to_z(s):
        return dev(wz(z + s), y, x, c)

    twin = dev(z, y, x, 1 - c)

    def rcopy(src, dst, ssem, rsem, device):
        return pltpu.make_async_remote_copy(
            src_ref=src, dst_ref=dst, send_sem=ssem, recv_sem=rsem,
            device_id=device, device_id_type=MESH,
        )

    barrier = pltpu.get_barrier_semaphore()
    for device in (twin, to_x(1), to_x(-1), to_y(1), to_y(-1), to_z(1), to_z(-1)):
        pl.semaphore_signal(barrier, inc=1, device_id=device, device_id_type=MESH)
    core_copy = pltpu.make_async_copy(cores_ref, core, core_sem)
    core_copy.start()
    for n in range(NQ):
        ag[n, y, x] = h_ref[:, n * CQ:(n + 1) * CQ]
        ag[NQ + n, y, x] = r_ref[:, n * CQ:(n + 1) * CQ]
    mb[0, y, x] = meta_ref[...]
    pl.semaphore_wait(barrier, 7)

    SIDES = ((0, 1), (0, -1), (1, 1), (1, -1))

    def ag_msg(n, kind, half, s):
        o = half * 64
        whole = pl.ds(o, 64)
        part = pl.ds(o + (0 if s > 0 else 32), 32)
        if kind == 0:
            ref = ag.at[n, y, x, whole]
        elif kind == 1:
            ref = ag.at[n, y, wx(x - s), part] if half == 0 else ag.at[n, wx(y - s), x, part]
        elif kind == 2:
            ref = ag.at[n, y, :, whole] if half == 0 else ag.at[n, :, x, whole]
        else:
            ref = ag.at[n, wx(y - s), :, part] if half == 0 else ag.at[n, :, wx(x - s), part]
        along_x = (half == 0) == (kind < 2)
        k = kind * 4 + half * 2 + (0 if s > 0 else 1)
        return rcopy(ref, ref, ag_s.at[n, k], ag_r.at[n, k], to_x(s) if along_x else to_y(s))

    def ag_own(n):
        for half, s in SIDES:
            ag_msg(n, 0, half, s).start()

    def ag_a(n):
        for half, s in SIDES:
            ag_msg(n, 0, half, s).wait_recv()
            ag_msg(n, 1, half, s).start()

    def ag_b(n):
        for half in (0, 1):
            for s in (1, -1):
                ag_msg(n, 1, half, s).wait_recv()
            for s in (1, -1):
                ag_msg(n, 2, half, s).start()

    def ag_c(n):
        for half, s in SIDES:
            ag_msg(n, 2, half, s).wait_recv()
            ag_msg(n, 3, half, s).start()

    def ag_d(n):
        for half, s in SIDES:
            ag_msg(n, 3, half, s).wait_recv()

    def mt_msg(k):
        if k < 2:
            ref, device = mb.at[0, y, x], to_x(1 if k == 0 else -1)
        elif k == 2:
            ref, device = mb.at[0, y, wx(x - 1)], to_x(1)
        elif k < 5:
            ref, device = mb.at[0, y], to_y(1 if k == 3 else -1)
        elif k == 5:
            ref, device = mb.at[0, wx(y - 1)], to_y(1)
        else:
            return rcopy(mb.at[0], mb.at[1], mt_s.at[k], mt_r.at[k], twin)
        return rcopy(ref, ref, mt_s.at[k], mt_r.at[k], device)

    def d2_msg(n):
        return rcopy(st.at[n], zc.at[n, 1], d2_s.at[n], d2_r.at[n], twin)

    def d2_back(b):
        k = 2 * NQ + b
        return rcopy(st.at[b], bk.at[b, pl.ds(2, 2)], d2_s.at[k], d2_r.at[k], twin)

    def build_slots():
        first = (y * NX + x) * 4
        names = []
        for o in range(4):
            e = first + 2 * c + o if o < 2 else first + 2 * (1 - c) + (o - 2)
            names.append(e.astype(F32))

        def assign(i, carry):
            rel = lax.div(i, NS)
            s = lax.rem(i, NS)
            tile = mb[rel, lax.div(s, NX), lax.rem(s, NX)].astype(F32)
            ids, gates = tile[0:8], tile[8:16]
            marks, weights = [], []
            for o in range(4):
                eq = ids == names[o]
                marks.append(jnp.sum(jnp.where(eq, 1.0, 0.0), axis=0, keepdims=True))
                weights.append(jnp.sum(jnp.where(eq, gates, 0.0), axis=0, keepdims=True))
            pad = jnp.zeros((4, TOK), F32)
            at = pl.ds(pl.multiple_of(i * 8, 8), 8)
            asg[at, :] = jnp.concatenate(marks + [pad], axis=0)
            gts[at, :] = jnp.concatenate(weights + [pad], axis=0)
            return carry

        lax.fori_loop(0, 2 * NS, assign, 0)
        before = (
            lax.broadcasted_iota(jnp.int32, (TOK, TOK), 0)
            < lax.broadcasted_iota(jnp.int32, (TOK, TOK), 1)
        )
        upper = jnp.where(before, 1.0, 0.0).astype(BF16)
        marks = asg[...]
        places = jnp.dot(marks.astype(BF16), upper, preferred_element_type=F32)
        code[...] = jnp.where(marks > 0.5, places, -1.0)
        slot = lax.broadcasted_iota(jnp.int32, (CAP, TOK), 0).astype(F32)

        def choose(s, carry):
            rows = code[pl.ds(pl.multiple_of(s * 8, 8), 8), :]
            hot = jnp.concatenate(
                [
                    jnp.where(jnp.broadcast_to(rows[o:o + 1], (CAP, TOK)) == slot, 1.0, 0.0)
                    for o in range(4)
                ],
                axis=0,
            )
            sel[s] = hot.astype(BF16)
            selt[s] = hot.T.astype(BF16)
            return carry

        lax.fori_loop(0, NS, choose, 0)

        def weigh(i, carry):
            rel = lax.div(i, NS)
            s = lax.rem(i, NS)
            at = pl.ds(pl.multiple_of(i * 8, 8), 8)
            rows, weights = code[at, :], gts[at, :]
            for o in range(2):
                mine = jnp.where(
                    jnp.broadcast_to(rows[o:o + 1], (CAP, TOK)) == slot,
                    jnp.broadcast_to(weights[o:o + 1], (CAP, TOK)),
                    0.0,
                )
                total = jnp.sum(mine, axis=1, keepdims=True)
                gc[o, rel, pl.ds(pl.multiple_of(s * CAP, CAP), CAP), :] = jnp.broadcast_to(
                    total, (CAP, TOK)
                )
            return carry

        lax.fori_loop(0, 2 * NS, weigh, 0)

    def compact(n):
        def one(ys, carry):
            for xs in range(NX):
                s = ys * NX + xs
                rows = jnp.dot(sel[s], ag[n, ys, xs], preferred_element_type=F32).astype(BF16)
                zc[n, 0, 0, s] = rows[0:32]
                zc[n, 0, 1, s] = rows[32:64]
                st[n, 0, s] = rows[64:96]
                st[n, 1, s] = rows[96:128]
            return carry

        lax.fori_loop(0, NY, one, 0)

    def compute_h(n, first):
        compact(n)
        d2_msg(n).start()
        for rel in (0, 1):
            if rel == 1:
                d2_msg(n).wait_recv()
            at = pl.ds(rel * ROWS, ROWS)
            for e in (0, 1):
                rows = zc[n, rel, e].reshape(ROWS, CQ)
                zct[e, cols(n), at] = rows.T

                def grow(q, carry):
                    part = jnp.dot(
                        zc[n, rel, e].reshape(ROWS, CQ), core[e, cols(n), cols(q)],
                        preferred_element_type=F32,
                    )
                    gs[q, e, at, :] = part if first else gs[q, e, at, :] + part
                    return carry

                lax.fori_loop(0, NQ, grow, 0)

    def compute_r(q):
        n = NQ + q
        compact(n)
        d2_msg(n).start()
        step = 64
        for rel in (0, 1):
            if rel == 1:
                d2_msg(n).wait_recv()

            def lower(i, carry):
                for e in (0, 1):
                    at = pl.ds(pl.multiple_of(rel * ROWS + i * step, step), step)
                    up = gs[q, e, at, :]
                    r = zc[n, rel, e, pl.ds(i * 2, 2)].reshape(step, CQ).astype(F32)
                    g = gc[e, rel, pl.ds(pl.multiple_of(i * step, step), step), :]
                    g = jnp.concatenate([g, g], axis=1)
                    sig = jax.nn.sigmoid(up)
                    slope = sig * (1.0 + up * (1.0 - sig))
                    lw[q, e, at, :] = (r * g * slope).astype(BF16)
                return carry

            lax.fori_loop(0, ROWS // step, lower, 0)

        def term(i, carry):
            e, m = lax.div(i, 2), lax.rem(i, 2)
            at = pl.ds(pl.multiple_of(m * 512, 512), 512)
            gs[q, e, at, :] = jnp.dot(zct[e, at, :], lw[q, e], preferred_element_type=F32)
            return carry

        lax.fori_loop(0, 4, term, 0)

    def z_msg(q, k, s):
        i = 0 if s > 0 else 1
        src, dst = {
            1: (zs1, z1), 2: (z2p, z2), 3: (z2, z3), 4: (z3, z4),
        }[k]
        j = (k - 1) * 2 + i
        return rcopy(src.at[q, i], dst.at[q, i], z_s.at[q, j], z_r.at[q, j], to_z(s))

    def part_of(d):
        return pl.ds(pl.multiple_of(d * TOK, TOK), TOK)

    def z_step(k, q):
        if k == 5:
            total = gs[q, :, part_of(z), :]
            for i, s in ((0, 1), (1, -1)):
                z_msg(q, 4, s).wait_recv()
                total = total + z4[q, i].astype(F32)
            cg_ref[:, :, cols(q)] = total
            return
        for i, s in ((0, 1), (1, -1)):
            if k == 1:
                zs1[q, i] = gs[q, i, part_of(wz(z + 4)), :].astype(BF16)
            elif k == 2:
                z_msg(q, 1, s).wait_recv()
                at = part_of(wz(z + 3 * s))
                z2p[q, i, i] = (gs[q, i, at, :] + z1[q, i].astype(F32)).astype(BF16)
                z2p[q, i, 1 - i] = gs[q, 1 - i, at, :].astype(BF16)
            else:
                got = z2 if k == 3 else z3
                z_msg(q, k - 1, s).wait_recv()
                at = part_of(wz(z + (5 - k) * s))
                got[q, i] = (gs[q, :, at, :] + got[q, i].astype(F32)).astype(BF16)
            z_msg(q, k, s).start()

    def compute_b(b):
        for rel in (1, 0):
            def back(e, carry):
                total = None
                for q in range(NQ):
                    part = lax.dot_general(
                        lw[q, e, pl.ds(rel * ROWS, ROWS), :], core[e, cols(b), cols(q)],
                        (((1,), (1,)), ((), ())), preferred_element_type=F32,
                    )
                    total = part if total is None else total + part
                rows = total.astype(BF16).reshape(NS, CAP, CQ)
                if rel == 1:
                    st[b, e] = rows
                else:
                    bk[b, e] = rows
                return carry

            lax.fori_loop(0, 2, back, 0)
            if rel == 1:
                d2_back(b).start()
        d2_back(b).wait_recv()

        def scatter(ys, carry):
            for xs in range(NX):
                s = ys * NX + xs
                rows = bk[b, :, s].reshape(4 * CAP, CQ)
                ag[b, ys, xs] = jnp.dot(selt[s], rows, preferred_element_type=F32).astype(BF16)
            return carry

        lax.fori_loop(0, NY, scatter, 0)

    def rs_msg(b, k, half, s):
        i = 0 if s > 0 else 1
        o = half * 64
        whole = pl.ds(o, 64)
        part = pl.ds(o + 32 * i, 32)
        if k == 1:
            src = ag.at[b, wx(y + 2), :, part] if half == 0 else ag.at[b, :, wx(x + 2), part]
            dst = rs1
        elif k == 2:
            src = ag.at[b, wx(y + s), :, whole] if half == 0 else ag.at[b, :, wx(x + s), whole]
            dst = rs2
        elif k == 3:
            src = ag.at[b, y, wx(x + 2), part] if half == 0 else ag.at[b, wx(y + 2), x, part]
            dst = rs3
        else:
            src = ag.at[b, y, wx(x + s), whole] if half == 0 else ag.at[b, wx(y + s), x, whole]
            dst = rs4
        along_y = (half == 0) == (k < 3)
        j = (k - 1) * 4 + half * 2 + i
        return rcopy(
            src, dst.at[b, half, i], rs_s.at[b, j], rs_r.at[b, j], to_y(s) if along_y else to_x(s)
        )

    def rs_step(k, b):
        for half in (0, 1):
            o = half * 64
            whole = pl.ds(o, 64)
            if k == 2 or k == 4:
                for i, s in ((0, 1), (1, -1)):
                    rs_msg(b, k - 1, half, s).wait_recv()
                    part = pl.ds(o + 32 * i, 32)
                    if k == 4:
                        yy, xx = (y, wx(x + s)) if half == 0 else (wx(y + s), x)
                        ag[b, yy, xx, part] = (
                            ag[b, yy, xx, part].astype(F32) + rs3[b, half, i].astype(F32)
                        ).astype(BF16)
                    else:
                        def add(j, carry):
                            yy, xx = (wx(y + s), j) if half == 0 else (j, wx(x + s))
                            ag[b, yy, xx, part] = (
                                ag[b, yy, xx, part].astype(F32) + rs1[b, half, i, j].astype(F32)
                            ).astype(BF16)
                            return carry

                        lax.fori_loop(0, 4, add, 0)
                    rs_msg(b, k, half, s).start()
            elif k == 3:
                for s in (1, -1):
                    rs_msg(b, 2, half, s).wait_recv()

                def merge(j, carry):
                    yy, xx = (y, j) if half == 0 else (j, x)
                    ag[b, yy, xx, whole] = (
                        ag[b, yy, xx, whole].astype(F32)
                        + rs2[b, half, 0, j].astype(F32)
                        + rs2[b, half, 1, j].astype(F32)
                    ).astype(BF16)
                    return carry

                lax.fori_loop(0, 4, merge, 0)
                for s in (1, -1):
                    rs_msg(b, 3, half, s).start()
            elif k == 1:
                for s in (1, -1):
                    rs_msg(b, 1, half, s).start()
            else:
                for s in (1, -1):
                    rs_msg(b, 4, half, s).wait_recv()
                rig_ref[whole, cols(b)] = (
                    ag[b, y, x, whole].astype(F32)
                    + rs4[b, half, 0].astype(F32)
                    + rs4[b, half, 1].astype(F32)
                ).astype(BF16)

    mt_msg(0).start()
    mt_msg(1).start()
    ag_own(0)
    ag_own(1)
    mt_msg(0).wait_recv()
    mt_msg(2).start()
    mt_msg(1).wait_recv()
    ag_a(0)
    mt_msg(2).wait_recv()
    mt_msg(3).start()
    mt_msg(4).start()
    ag_b(0)
    ag_a(1)
    mt_msg(3).wait_recv()
    mt_msg(5).start()
    mt_msg(4).wait_recv()
    ag_b(1)

    def tick_comm(n, more, extra=None):
        ag_c(n)

        def ahead():
            ag_own(n + 2)
            ag_a(n + 2)
            ag_b(n + 2)

        when(more, ahead)
        if extra is not None:
            extra()
        ag_d(n)

    def meta_ready():
        mt_msg(5).wait_recv()
        mt_msg(6).start()
        mt_msg(6).wait_recv()
        build_slots()
        core_copy.wait()

    tick_comm(0, True, meta_ready)
    compute_h(0, True)

    def h_tick(n, carry):
        tick_comm(n, True)
        compute_h(n, False)
        return carry

    lax.fori_loop(1, NQ, h_tick, 0)

    def r_tick(q, carry):
        def chains():
            for k in (4, 3, 2):
                when(q >= k - 1, lambda k=k: z_step(k, q - (k - 1)))

        tick_comm(NQ + q, q < 2, chains)
        compute_r(q)
        z_step(1, q)
        return carry

    lax.fori_loop(0, NQ, r_tick, 0)

    def sent(n, carry):
        for kind in range(4):
            for half, s in SIDES:
                ag_msg(n, kind, half, s).wait_send()
        d2_msg(n).wait_send()
        return carry

    lax.fori_loop(0, 2 * NQ, sent, 0)

    def tail(t, carry):
        def fresh():
            compute_b(t)
            rs_step(1, t)

        when(t < NQ, fresh)
        for k in (5, 4, 3, 2):
            when((t >= k - 1) & (t < NQ + k - 1), lambda k=k: rs_step(k, t - (k - 1)))
        for k in (5, 4, 3, 2):
            when(t < k - 1, lambda k=k: z_step(k, t + 5 - k))
        return carry

    lax.fori_loop(0, NQ + 4, tail, 0)

    for k in range(7):
        mt_msg(k).wait_send()

    def flushed(q, carry):
        d2_back(q).wait_send()
        for k in range(1, 5):
            for s in (1, -1):
                z_msg(q, k, s).wait_send()
            for half, s in SIDES:
                rs_msg(q, k, half, s).wait_send()
        return carry

    lax.fori_loop(0, NQ, flushed, 0)


def local(hidden_in, rank_grad, gates, expert_ids, cores):
    meta = jnp.concatenate([expert_ids.T.astype(BF16), gates.T], axis=0)
    vmem = pl.BlockSpec(memory_space=pltpu.VMEM)
    dma = pltpu.SemaphoreType.DMA
    rig, cg = pl.pallas_call(
        body,
        out_shape=(
            jax.ShapeDtypeStruct((TOK, NQ * CQ), BF16),
            jax.ShapeDtypeStruct((2, TOK, NQ * CQ), F32),
        ),
        in_specs=[vmem, vmem, vmem, pl.BlockSpec(memory_space=pl.ANY)],
        out_specs=(vmem, vmem),
        scratch_shapes=[
            pltpu.VMEM((2 * NQ, NY, NX, TOK, CQ), BF16),
            pltpu.VMEM((2, NY, NX, 16, TOK), BF16),
            pltpu.VMEM((2, NQ * CQ, NQ * CQ), BF16),
            pltpu.VMEM((2 * NQ, 2, 2, NS, CAP, CQ), BF16),
            pltpu.VMEM((2 * NQ, 2, NS, CAP, CQ), BF16),
            pltpu.VMEM((NQ, 2, 2 * ROWS, CQ), F32),
            pltpu.VMEM((NQ, 2, 2 * ROWS, CQ), BF16),
            pltpu.VMEM((2, NQ * CQ, 2 * ROWS), BF16),
            pltpu.VMEM((NQ, 4, NS, CAP, CQ), BF16),
            pltpu.VMEM((NS, 4 * CAP, TOK), BF16),
            pltpu.VMEM((NS, TOK, 4 * CAP), BF16),
            pltpu.VMEM((2, 2, ROWS, TOK), F32),
            pltpu.VMEM((2 * NS * 8, TOK), F32),
            pltpu.VMEM((2 * NS * 8, TOK), F32),
            pltpu.VMEM((2 * NS * 8, TOK), F32),
            pltpu.VMEM((NQ, 2, TOK, CQ), BF16),
            pltpu.VMEM((NQ, 2, TOK, CQ), BF16),
            pltpu.VMEM((NQ, 2, 2, TOK, CQ), BF16),
            pltpu.VMEM((NQ, 2, 2, TOK, CQ), BF16),
            pltpu.VMEM((NQ, 2, 2, TOK, CQ), BF16),
            pltpu.VMEM((NQ, 2, 2, TOK, CQ), BF16),
            pltpu.VMEM((NQ, 2, 2, 4, 32, CQ), BF16),
            pltpu.VMEM((NQ, 2, 2, 4, 64, CQ), BF16),
            pltpu.VMEM((NQ, 2, 2, 32, CQ), BF16),
            pltpu.VMEM((NQ, 2, 2, 64, CQ), BF16),
            dma, dma((2 * NQ, 16)), dma((2 * NQ, 16)), dma((7,)), dma((7,)),
            dma((3 * NQ,)), dma((3 * NQ,)), dma((NQ, 8)), dma((NQ, 8)),
            dma((NQ, 16)), dma((NQ, 16)),
        ],
        compiler_params=pltpu.CompilerParams(
            collective_id=0, has_side_effects=True, vmem_limit_bytes=62 * 1024 * 1024
        ),
        cost_estimate=pl.CostEstimate(
            flops=14_000_000_000, bytes_accessed=8_000_000, transcendentals=2_000_000
        ),
        name="moe_core_backward",
    )(hidden_in, rank_grad, meta, cores)
    return rig, jnp.transpose(cg, (1, 0, 2))


def solution(mesh):
    in_specs = (
        P(("dp", "expert"), None),
        P(("dp", "expert"), None),
        P(("dp", "expert"), None),
        P(("dp", "expert"), None),
        P("expert", None, None),
    )
    out_specs = (P(("dp", "expert"), None), P("dp", "expert", None))
    return jax.shard_map(local, mesh=mesh, in_specs=in_specs, out_specs=out_specs, check_vma=False)
```

```python
import jax
import jax.numpy as jnp
from jax import lax
from jax.experimental import pallas as pl
from jax.experimental.pallas import tpu as pltpu
from jax.sharding import PartitionSpec as P

MESH = pl.DeviceIdType.MESH
F32 = jnp.float32
BF16 = jnp.bfloat16
NZ, NY, NX = 8, 4, 4
CQ = 256
NQ = 4
TOK = 128
CAP = 32
NS = NY * NX
ROWS = NS * CAP


def when(cond, fn):
    if isinstance(cond, bool):
        if cond:
            fn()
    else:
        pl.when(cond)(fn)


def cols(i):
    if isinstance(i, int):
        return pl.ds(i * CQ, CQ)
    return pl.ds(pl.multiple_of(i * CQ, CQ), CQ)


def body(
    h_ref, r_ref, meta_ref, cores_ref,
    rig_ref, cg_ref,
    ag, mb, core, zc, st, gs, lw, zct, bk, sel, selt, gc, asg, code, gts,
    z1, zs1, z2p, z2, z3, z4, rs1, rs2, rs3,
    core_sem, p1_s, p1_r, ag_s, ag_r, mt_s, mt_r, d2_s, d2_r, z_s, z_r, rs_s, rs_r,
):
    z = lax.axis_index("dp")
    ei = lax.axis_index("expert")
    c = lax.rem(ei, 2)
    x = lax.rem(lax.div(ei, 2), NX)
    y = lax.div(ei, 2 * NX)

    def wx(v):
        return lax.rem(v + NX, NX)

    def wz(v):
        return lax.rem(v + NZ, NZ)

    def dev(zz, yy, xx, cc):
        return (zz, (yy * NX + xx) * 2 + cc)

    def to_x(s):
        return dev(z, y, wx(x + s), c)

    def to_y(s):
        return dev(z, wx(y + s), x, c)

    def to_z(s):
        return dev(wz(z + s), y, x, c)

    twin = dev(z, y, x, 1 - c)

    def rcopy(src, dst, ssem, rsem, device):
        return pltpu.make_async_remote_copy(
            src_ref=src, dst_ref=dst, send_sem=ssem, recv_sem=rsem,
            device_id=device, device_id_type=MESH,
        )

    barrier = pltpu.get_barrier_semaphore()
    for device in (
        twin, to_x(1), to_x(-1), to_x(2), to_y(1), to_y(-1), to_y(2), to_z(1), to_z(-1)
    ):
        pl.semaphore_signal(barrier, inc=1, device_id=device, device_id_type=MESH)
    core_copy = pltpu.make_async_copy(cores_ref, core, core_sem)
    core_copy.start()
    for n in range(NQ):
        ag[n, y, x] = h_ref[:, n * CQ:(n + 1) * CQ]
    mb[0, y, x] = meta_ref[...]
    pl.semaphore_wait(barrier, 9)

    SIDES = ((0, 1), (0, -1), (1, 1), (1, -1))
    HOPS = (1, -1, 2)
    GROUPS = ((0, 1), (1, NQ - 1), (NQ, NQ))

    def near_msg(g, half, j):
        lo, count = GROUPS[g]
        ref = ag.at[pl.ds(lo, count), y, x, pl.ds(half * 64, 64)]
        k = half * 3 + j
        device = to_x(HOPS[j]) if half == 0 else to_y(HOPS[j])
        return rcopy(ref, ref, p1_s.at[g, k], p1_r.at[g, k], device)

    def near(g, act):
        for half in (0, 1):
            for j in range(3):
                getattr(near_msg(g, half, j), act)()

    def ag_msg(n, kind, half, s):
        o = half * 64
        whole = pl.ds(o, 64)
        part = pl.ds(o + (0 if s > 0 else 32), 32)
        if kind == 0:
            ref = ag.at[n, y, :, whole] if half == 0 else ag.at[n, :, x, whole]
        else:
            ref = ag.at[n, wx(y - s), :, part] if half == 0 else ag.at[n, :, wx(x - s), part]
        k = kind * 4 + half * 2 + (0 if s > 0 else 1)
        return rcopy(
            ref, ref, ag_s.at[n, k], ag_r.at[n, k], to_y(s) if half == 0 else to_x(s)
        )

    def ag_own(n):
        for half, s in SIDES:
            ag_msg(n, 0, half, s).start()

    def ag_on(n):
        for half, s in SIDES:
            ag_msg(n, 0, half, s).wait_recv()
            ag_msg(n, 1, half, s).start()

    def ag_done(n):
        for half, s in SIDES:
            ag_msg(n, 1, half, s).wait_recv()

    def mt_msg(k):
        if k < 3:
            ref, device = mb.at[0, y, x], to_x(HOPS[k])
        elif k < 6:
            ref, device = mb.at[0, y], to_y(HOPS[k - 3])
        else:
            return rcopy(mb.at[0], mb.at[1], mt_s.at[k], mt_r.at[k], twin)
        return rcopy(ref, ref, mt_s.at[k], mt_r.at[k], device)

    def d2_msg(n):
        return rcopy(st.at[n], zc.at[n, 1], d2_s.at[n], d2_r.at[n], twin)

    def d2_back(b):
        k = 2 * NQ + b
        return rcopy(st.at[b], bk.at[b, pl.ds(2, 2)], d2_s.at[k], d2_r.at[k], twin)

    def build_slots():
        first = (y * NX + x) * 4
        names = []
        for o in range(4):
            e = first + 2 * c + o if o < 2 else first + 2 * (1 - c) + (o - 2)
            names.append(e.astype(F32))

        def assign(i, carry):
            rel = lax.div(i, NS)
            s = lax.rem(i, NS)
            tile = mb[rel, lax.div(s, NX), lax.rem(s, NX)].astype(F32)
            ids, gates = tile[0:8], tile[8:16]
            marks, weights = [], []
            for o in range(4):
                eq = ids == names[o]
                marks.append(jnp.sum(jnp.where(eq, 1.0, 0.0), axis=0, keepdims=True))
                weights.append(jnp.sum(jnp.where(eq, gates, 0.0), axis=0, keepdims=True))
            pad = jnp.zeros((4, TOK), F32)
            at = pl.ds(pl.multiple_of(i * 8, 8), 8)
            asg[at, :] = jnp.concatenate(marks + [pad], axis=0)
            gts[at, :] = jnp.concatenate(weights + [pad], axis=0)
            return carry

        lax.fori_loop(0, 2 * NS, assign, 0)
        before = (
            lax.broadcasted_iota(jnp.int32, (TOK, TOK), 0)
            < lax.broadcasted_iota(jnp.int32, (TOK, TOK), 1)
        )
        upper = jnp.where(before, 1.0, 0.0).astype(BF16)
        marks = asg[...]
        places = jnp.dot(marks.astype(BF16), upper, preferred_element_type=F32)
        code[...] = jnp.where(marks > 0.5, places, -1.0)
        slot = lax.broadcasted_iota(jnp.int32, (CAP, TOK), 0).astype(F32)

        def choose(s, carry):
            rows = code[pl.ds(pl.multiple_of(s * 8, 8), 8), :]
            hot = jnp.concatenate(
                [
                    jnp.where(jnp.broadcast_to(rows[o:o + 1], (CAP, TOK)) == slot, 1.0, 0.0)
                    for o in range(4)
                ],
                axis=0,
            )
            sel[s] = hot.astype(BF16)
            selt[s] = hot.T.astype(BF16)
            return carry

        lax.fori_loop(0, NS, choose, 0)

    def build_gates():
        slot = lax.broadcasted_iota(jnp.int32, (CAP, TOK), 0).astype(F32)

        def weigh(i, carry):
            rel = lax.div(i, NS)
            s = lax.rem(i, NS)
            at = pl.ds(pl.multiple_of(i * 8, 8), 8)
            rows, weights = code[at, :], gts[at, :]
            for o in range(2):
                mine = jnp.where(
                    jnp.broadcast_to(rows[o:o + 1], (CAP, TOK)) == slot,
                    jnp.broadcast_to(weights[o:o + 1], (CAP, TOK)),
                    0.0,
                )
                total = jnp.sum(mine, axis=1, keepdims=True)
                gc[o, rel, pl.ds(pl.multiple_of(s * CAP, CAP), CAP), :] = jnp.broadcast_to(
                    total, (CAP, TOK)
                )
            return carry

        lax.fori_loop(0, 2 * NS, weigh, 0)

    def compact(n):
        def one(ys, carry):
            for xs in range(NX):
                s = ys * NX + xs
                rows = jnp.dot(sel[s], ag[n, ys, xs], preferred_element_type=F32).astype(BF16)
                zc[n, 0, 0, s] = rows[0:32]
                zc[n, 0, 1, s] = rows[32:64]
                st[n, 0, s] = rows[64:96]
                st[n, 1, s] = rows[96:128]
            return carry

        lax.fori_loop(0, NY, one, 0)

    def turn(n, rel):
        for e in (0, 1):
            zct[e, cols(n), pl.ds(rel * ROWS, ROWS)] = zc[n, rel, e].reshape(ROWS, CQ).T

    def compute_h(n):
        compact(n)
        d2_msg(n).start()
        turn(n, 0)

        def other():
            d2_msg(n - 1).wait_recv()
            turn(n - 1, 1)

        when(n >= 1, other)

    def compute_upper(q):
        def one(i, carry):
            e, rel = lax.div(i, 2), lax.rem(i, 2)
            total = None
            for n in range(NQ):
                part = jnp.dot(
                    zc[n, rel, e].reshape(ROWS, CQ), core[e, cols(n), cols(q)],
                    preferred_element_type=F32,
                )
                total = part if total is None else total + part
            gs[q, e, pl.ds(pl.multiple_of(rel * ROWS, ROWS), ROWS), :] = total
            return carry

        lax.fori_loop(0, 4, one, 0)

    def compute_r(q):
        n = NQ + q
        compact(n)
        d2_msg(n).start()
        step = 64
        for rel in (0, 1):
            if rel == 1:
                d2_msg(n).wait_recv()

            def lower(i, carry):
                for e in (0, 1):
                    at = pl.ds(pl.multiple_of(rel * ROWS + i * step, step), step)
                    up = gs[q, e, at, :]
                    r = zc[n, rel, e, pl.ds(i * 2, 2)].reshape(step, CQ).astype(F32)
                    g = gc[e, rel, pl.ds(pl.multiple_of(i * step, step), step), :]
                    g = jnp.concatenate([g, g], axis=1)
                    sig = jax.nn.sigmoid(up)
                    slope = sig * (1.0 + up * (1.0 - sig))
                    lw[q, e, at, :] = (r * g * slope).astype(BF16)
                return carry

            lax.fori_loop(0, ROWS // step, lower, 0)

        def term(i, carry):
            e, m = lax.div(i, 2), lax.rem(i, 2)
            at = pl.ds(pl.multiple_of(m * 512, 512), 512)
            gs[q, e, at, :] = jnp.dot(zct[e, at, :], lw[q, e], preferred_element_type=F32)
            return carry

        lax.fori_loop(0, 4, term, 0)

    def z_msg(q, k, s):
        i = 0 if s > 0 else 1
        src, dst = {
            1: (zs1, z1), 2: (z2p, z2), 3: (z2, z3), 4: (z3, z4),
        }[k]
        j = (k - 1) * 2 + i
        return rcopy(src.at[q, i], dst.at[q, i], z_s.at[q, j], z_r.at[q, j], to_z(s))

    def part_of(d):
        return pl.ds(pl.multiple_of(d * TOK, TOK), TOK)

    def z_step(k, q):
        if k == 5:
            total = gs[q, :, part_of(z), :]
            for i, s in ((0, 1), (1, -1)):
                z_msg(q, 4, s).wait_recv()
                total = total + z4[q, i].astype(F32)
            cg_ref[:, :, cols(q)] = total
            return
        for i, s in ((0, 1), (1, -1)):
            if k == 1:
                zs1[q, i] = gs[q, i, part_of(wz(z + 4)), :].astype(BF16)
            elif k == 2:
                z_msg(q, 1, s).wait_recv()
                at = part_of(wz(z + 3 * s))
                z2p[q, i, i] = (gs[q, i, at, :] + z1[q, i].astype(F32)).astype(BF16)
                z2p[q, i, 1 - i] = gs[q, 1 - i, at, :].astype(BF16)
            else:
                got = z2 if k == 3 else z3
                z_msg(q, k - 1, s).wait_recv()
                at = part_of(wz(z + (5 - k) * s))
                got[q, i] = (gs[q, :, at, :] + got[q, i].astype(F32)).astype(BF16)
            z_msg(q, k, s).start()

    def compute_b(b):
        for rel in (1, 0):
            def back(e, carry):
                total = None
                for q in range(NQ):
                    part = lax.dot_general(
                        lw[q, e, pl.ds(rel * ROWS, ROWS), :], core[e, cols(b), cols(q)],
                        (((1,), (1,)), ((), ())), preferred_element_type=F32,
                    )
                    total = part if total is None else total + part
                rows = total.astype(BF16).reshape(NS, CAP, CQ)
                if rel == 1:
                    st[b, e] = rows
                else:
                    bk[b, e] = rows
                return carry

            lax.fori_loop(0, 2, back, 0)
            if rel == 1:
                d2_back(b).start()
        d2_back(b).wait_recv()

        def scatter(ys, carry):
            for xs in range(NX):
                s = ys * NX + xs
                rows = bk[b, :, s].reshape(4 * CAP, CQ)
                ag[b, ys, xs] = jnp.dot(selt[s], rows, preferred_element_type=F32).astype(BF16)
            return carry

        lax.fori_loop(0, NY, scatter, 0)

    def rs_msg(b, k, half, s):
        i = 0 if s > 0 else 1
        o = half * 64
        whole = pl.ds(o, 64)
        part = pl.ds(o + 32 * i, 32)
        if k == 1:
            src = ag.at[b, wx(y + 2), :, part] if half == 0 else ag.at[b, :, wx(x + 2), part]
            dst = rs1
        else:
            src = ag.at[b, wx(y + s), :, whole] if half == 0 else ag.at[b, :, wx(x + s), whole]
            dst = rs2
        j = (k - 1) * 4 + half * 2 + i
        return rcopy(
            src, dst.at[b, half, i], rs_s.at[b, j], rs_r.at[b, j], to_y(s) if half == 0 else to_x(s)
        )

    def last_msg(b, half, j):
        whole = pl.ds(half * 64, 64)
        s = HOPS[j]
        src = ag.at[b, y, wx(x + s), whole] if half == 0 else ag.at[b, wx(y + s), x, whole]
        k = 8 + half * 3 + j
        return rcopy(
            src, rs3.at[b, half, j], rs_s.at[b, k], rs_r.at[b, k], to_x(s) if half == 0 else to_y(s)
        )

    def rs_step(k, b):
        for half in (0, 1):
            o = half * 64
            whole = pl.ds(o, 64)
            if k == 1:
                for s in (1, -1):
                    rs_msg(b, 1, half, s).start()
            elif k == 2:
                for i, s in ((0, 1), (1, -1)):
                    rs_msg(b, 1, half, s).wait_recv()
                    part = pl.ds(o + 32 * i, 32)

                    def add(j, carry):
                        yy, xx = (wx(y + s), j) if half == 0 else (j, wx(x + s))
                        ag[b, yy, xx, part] = (
                            ag[b, yy, xx, part].astype(F32) + rs1[b, half, i, j].astype(F32)
                        ).astype(BF16)
                        return carry

                    lax.fori_loop(0, 4, add, 0)
                    rs_msg(b, 2, half, s).start()
            elif k == 3:
                for s in (1, -1):
                    rs_msg(b, 2, half, s).wait_recv()

                def merge(j, carry):
                    yy, xx = (y, j) if half == 0 else (j, x)
                    ag[b, yy, xx, whole] = (
                        ag[b, yy, xx, whole].astype(F32)
                        + rs2[b, half, 0, j].astype(F32)
                        + rs2[b, half, 1, j].astype(F32)
                    ).astype(BF16)
                    return carry

                lax.fori_loop(0, 4, merge, 0)
                for j in range(3):
                    last_msg(b, half, j).start()
            else:
                total = ag[b, y, x, whole].astype(F32)
                for j in range(3):
                    last_msg(b, half, j).wait_recv()
                    total = total + rs3[b, half, j].astype(F32)
                rig_ref[whole, cols(b)] = total.astype(BF16)

    near(0, "start")
    for k in range(3):
        mt_msg(k).start()
    near(1, "start")
    for n in range(NQ):
        ag[NQ + n, y, x] = r_ref[:, n * CQ:(n + 1) * CQ]
    for k in range(3):
        mt_msg(k).wait_recv()
    for k in range(3, 6):
        mt_msg(k).start()
    near(0, "wait_recv")
    ag_own(0)
    near(1, "wait_recv")
    ag_own(1)
    for k in range(3, 6):
        mt_msg(k).wait_recv()
    mt_msg(6).start()
    mt_msg(6).wait_recv()
    build_slots()
    core_copy.wait()
    ag_on(0)
    ag_own(2)
    near(2, "start")

    def h_tick(n, carry):
        ag_on(n)
        when(n == 2, lambda: near(2, "wait_recv"))
        ag_own(n + 2)
        ag_done(n - 1)
        compute_h(n - 1)
        return carry

    lax.fori_loop(1, NQ + 1, h_tick, 0)
    build_gates()
    d2_msg(NQ - 1).wait_recv()
    turn(NQ - 1, 1)

    def r_tick(q, carry):
        n = NQ + 1 + q
        when(q < NQ - 1, lambda: ag_on(n))
        when(q < 1, lambda: ag_own(n + 2))
        compute_upper(q)
        for k in (4, 3, 2):
            when(q >= k - 1, lambda k=k: z_step(k, q - (k - 1)))
        ag_done(n - 1)
        compute_r(q)
        z_step(1, q)
        return carry

    lax.fori_loop(0, NQ, r_tick, 0)

    def sent(n, carry):
        for kind in range(2):
            for half, s in SIDES:
                ag_msg(n, kind, half, s).wait_send()
        d2_msg(n).wait_send()
        return carry

    lax.fori_loop(0, 2 * NQ, sent, 0)
    for g in range(3):
        near(g, "wait_send")

    def tail(t, carry):
        def fresh():
            compute_b(t)
            rs_step(1, t)

        when(t < NQ, fresh)
        for k in (4, 3, 2):
            when((t >= k - 1) & (t < NQ + k - 1), lambda k=k: rs_step(k, t - (k - 1)))
        for k in (5, 4, 3, 2):
            when(t < k - 1, lambda k=k: z_step(k, t + 5 - k))
        return carry

    lax.fori_loop(0, NQ + 3, tail, 0)

    for k in range(7):
        mt_msg(k).wait_send()

    def flushed(q, carry):
        d2_back(q).wait_send()
        for k in range(1, 5):
            for s in (1, -1):
                z_msg(q, k, s).wait_send()
        for half, s in SIDES:
            for k in (1, 2):
                rs_msg(q, k, half, s).wait_send()
        for half in (0, 1):
            for j in range(3):
                last_msg(q, half, j).wait_send()
        return carry

    lax.fori_loop(0, NQ, flushed, 0)


def local(hidden_in, rank_grad, gates, expert_ids, cores):
    meta = jnp.concatenate([expert_ids.T.astype(BF16), gates.T], axis=0)
    vmem = pl.BlockSpec(memory_space=pltpu.VMEM)
    dma = pltpu.SemaphoreType.DMA
    rig, cg = pl.pallas_call(
        body,
        out_shape=(
            jax.ShapeDtypeStruct((TOK, NQ * CQ), BF16),
            jax.ShapeDtypeStruct((2, TOK, NQ * CQ), F32),
        ),
        in_specs=[vmem, vmem, vmem, pl.BlockSpec(memory_space=pl.ANY)],
        out_specs=(vmem, vmem),
        scratch_shapes=[
            pltpu.VMEM((2 * NQ, NY, NX, TOK, CQ), BF16),
            pltpu.VMEM((2, NY, NX, 16, TOK), BF16),
            pltpu.VMEM((2, NQ * CQ, NQ * CQ), BF16),
            pltpu.VMEM((2 * NQ, 2, 2, NS, CAP, CQ), BF16),
            pltpu.VMEM((2 * NQ, 2, NS, CAP, CQ), BF16),
            pltpu.VMEM((NQ, 2, 2 * ROWS, CQ), F32),
            pltpu.VMEM((NQ, 2, 2 * ROWS, CQ), BF16),
            pltpu.VMEM((2, NQ * CQ, 2 * ROWS), BF16),
            pltpu.VMEM((NQ, 4, NS, CAP, CQ), BF16),
            pltpu.VMEM((NS, 4 * CAP, TOK), BF16),
            pltpu.VMEM((NS, TOK, 4 * CAP), BF16),
            pltpu.VMEM((2, 2, ROWS, TOK), F32),
            pltpu.VMEM((2 * NS * 8, TOK), F32),
            pltpu.VMEM((2 * NS * 8, TOK), F32),
            pltpu.VMEM((2 * NS * 8, TOK), F32),
            pltpu.VMEM((NQ, 2, TOK, CQ), BF16),
            pltpu.VMEM((NQ, 2, TOK, CQ), BF16),
            pltpu.VMEM((NQ, 2, 2, TOK, CQ), BF16),
            pltpu.VMEM((NQ, 2, 2, TOK, CQ), BF16),
            pltpu.VMEM((NQ, 2, 2, TOK, CQ), BF16),
            pltpu.VMEM((NQ, 2, 2, TOK, CQ), BF16),
            pltpu.VMEM((NQ, 2, 2, 4, 32, CQ), BF16),
            pltpu.VMEM((NQ, 2, 2, 4, 64, CQ), BF16),
            pltpu.VMEM((NQ, 2, 3, 64, CQ), BF16),
            dma, dma((3, 6)), dma((3, 6)), dma((2 * NQ, 8)), dma((2 * NQ, 8)), dma((7,)), dma((7,)),
            dma((3 * NQ,)), dma((3 * NQ,)), dma((NQ, 8)), dma((NQ, 8)),
            dma((NQ, 14)), dma((NQ, 14)),
        ],
        compiler_params=pltpu.CompilerParams(
            collective_id=0, has_side_effects=True, vmem_limit_bytes=62 * 1024 * 1024
        ),
        cost_estimate=pl.CostEstimate(
            flops=14_000_000_000, bytes_accessed=8_000_000, transcendentals=2_000_000
        ),
        name="moe_core_backward",
    )(hidden_in, rank_grad, meta, cores)
    return rig, jnp.transpose(cg, (1, 0, 2))


def solution(mesh):
    in_specs = (
        P(("dp", "expert"), None),
        P(("dp", "expert"), None),
        P(("dp", "expert"), None),
        P(("dp", "expert"), None),
        P("expert", None, None),
    )
    out_specs = (P(("dp", "expert"), None), P("dp", "expert", None))
    return jax.shard_map(local, mesh=mesh, in_specs=in_specs, out_specs=out_specs, check_vma=False)
```

```python
import jax
import jax.numpy as jnp
from jax import lax
from jax.experimental import pallas as pl
from jax.experimental.pallas import tpu as pltpu
from jax.sharding import PartitionSpec as P

MESH = pl.DeviceIdType.MESH
F32 = jnp.float32
BF16 = jnp.bfloat16
NZ, NY, NX = 8, 4, 4
CQ = 256
NQ = 4
TOK = 128
CAP = 32
NS = NY * NX
ROWS = NS * CAP


ORDER = (
    ("o", 5), ("u", 0), ("u", 1), ("o", 6), ("c", 0), ("k", 0), ("c", 1), ("o", 7), ("k", 1),
    ("l", 0), ("t", 0), ("z1", 0), ("l", 1), ("t", 1), ("z1", 1), ("c", 2), ("z2", 0), ("c", 3),
    ("u", 2), ("z2", 1), ("u", 3), ("k", 3), ("z3", 0), ("k", 2), ("l", 2), ("l", 3), ("b", 0),
    ("a", 0), ("z3", 1), ("b", 1), ("a", 1), ("s", 0), ("r1", 0), ("z4", 0), ("t", 3),
    ("z1", 3), ("z4", 1), ("s", 1), ("r1", 1), ("r2", 0), ("t", 2), ("z1", 2), ("z2", 3),
    ("b", 2), ("r2", 1), ("a", 2), ("b", 3), ("r3", 0), ("z2", 2), ("s", 2), ("r1", 2),
    ("a", 3), ("r3", 1), ("z3", 3), ("s", 3), ("r1", 3), ("r4", 0), ("z5", 0), ("r2", 2),
    ("z3", 2), ("z5", 1), ("r4", 1), ("r2", 3), ("z4", 3), ("r3", 2), ("z4", 2), ("r3", 3),
    ("z5", 3), ("r4", 2), ("z5", 2), ("r4", 3),
)


def when(cond, fn):
    if isinstance(cond, bool):
        if cond:
            fn()
    else:
        pl.when(cond)(fn)


def cols(i):
    if isinstance(i, int):
        return pl.ds(i * CQ, CQ)
    return pl.ds(pl.multiple_of(i * CQ, CQ), CQ)


def body(
    h_ref, r_ref, ids_ref, gates_ref, cores_ref,
    rig_ref, cg_ref,
    ag, mb, core, zc, st, gs, lw, zct, bk, sel, selt, gc, asg, code, gts,
    z1, zs1, z2p, z2, z3, z4, rs1, rs2, rs3,
    core_sem, p1_s, p1_r, ag_s, ag_r, mt_s, mt_r, d2_s, d2_r, z_s, z_r, rs_s, rs_r,
):
    z = lax.axis_index("dp")
    ei = lax.axis_index("expert")
    c = lax.rem(ei, 2)
    x = lax.rem(lax.div(ei, 2), NX)
    y = lax.div(ei, 2 * NX)

    def wx(v):
        return lax.rem(v + NX, NX)

    def wz(v):
        return lax.rem(v + NZ, NZ)

    def dev(zz, yy, xx, cc):
        return (zz, (yy * NX + xx) * 2 + cc)

    def to_x(s):
        return dev(z, y, wx(x + s), c)

    def to_y(s):
        return dev(z, wx(y + s), x, c)

    def to_z(s):
        return dev(wz(z + s), y, x, c)

    twin = dev(z, y, x, 1 - c)

    def rcopy(src, dst, ssem, rsem, device):
        return pltpu.make_async_remote_copy(
            src_ref=src, dst_ref=dst, send_sem=ssem, recv_sem=rsem,
            device_id=device, device_id_type=MESH,
        )

    barrier = pltpu.get_barrier_semaphore()
    for device in (
        twin, to_x(1), to_x(-1), to_x(2), to_y(1), to_y(-1), to_y(2), to_z(1), to_z(-1)
    ):
        pl.semaphore_signal(barrier, inc=1, device_id=device, device_id_type=MESH)
    core_copy = pltpu.make_async_copy(cores_ref, core, core_sem)
    core_copy.start()
    for n in range(NQ):
        ag[n, y, x] = h_ref[:, n * CQ:(n + 1) * CQ]
    mb[0, y, x] = jnp.concatenate(
        [ids_ref[...].astype(F32), gates_ref[...].astype(F32)], axis=0
    ).astype(BF16)
    pl.semaphore_wait(barrier, 9)

    SIDES = ((0, 1), (0, -1), (1, 1), (1, -1))
    HOPS = (1, -1, 2)
    GROUPS = ((0, 1), (1, NQ - 1), (NQ, NQ))

    def near_msg(g, half, j):
        lo, count = GROUPS[g]
        ref = ag.at[pl.ds(lo, count), y, x, pl.ds(half * 64, 64)]
        k = half * 3 + j
        device = to_x(HOPS[j]) if half == 0 else to_y(HOPS[j])
        return rcopy(ref, ref, p1_s.at[g, k], p1_r.at[g, k], device)

    def near(g, act):
        for half in (0, 1):
            for j in range(3):
                getattr(near_msg(g, half, j), act)()

    def ag_msg(n, kind, half, s):
        o = half * 64
        whole = pl.ds(o, 64)
        part = pl.ds(o + (0 if s > 0 else 32), 32)
        if kind == 0:
            ref = ag.at[n, y, :, whole] if half == 0 else ag.at[n, :, x, whole]
        else:
            ref = ag.at[n, wx(y - s), :, part] if half == 0 else ag.at[n, :, wx(x - s), part]
        k = kind * 4 + half * 2 + (0 if s > 0 else 1)
        return rcopy(
            ref, ref, ag_s.at[n, k], ag_r.at[n, k], to_y(s) if half == 0 else to_x(s)
        )

    def ag_own(n):
        for half, s in SIDES:
            ag_msg(n, 0, half, s).start()

    def ag_on(n):
        for half, s in SIDES:
            ag_msg(n, 0, half, s).wait_recv()
            ag_msg(n, 1, half, s).start()

    def ag_done(n):
        for half, s in SIDES:
            ag_msg(n, 1, half, s).wait_recv()

    def mt_msg(k):
        if k < 3:
            ref, device = mb.at[0, y, x], to_x(HOPS[k])
        elif k < 6:
            ref, device = mb.at[0, y], to_y(HOPS[k - 3])
        else:
            return rcopy(mb.at[0], mb.at[1], mt_s.at[k], mt_r.at[k], twin)
        return rcopy(ref, ref, mt_s.at[k], mt_r.at[k], device)

    def d2_msg(n):
        return rcopy(st.at[n], zc.at[n, 1], d2_s.at[n], d2_r.at[n], twin)

    def d2_back(b):
        k = 2 * NQ + b
        return rcopy(st.at[b], bk.at[b, pl.ds(2, 2)], d2_s.at[k], d2_r.at[k], twin)

    def build_slots(rel):
        first = (y * NX + x) * 4
        names = []
        for o in range(4):
            e = first + 2 * c + o if o < 2 else first + 2 * (1 - c) + (o - 2)
            names.append(e.astype(F32))

        def assign(s, carry):
            i = rel * NS + s
            tile = mb[rel, lax.div(s, NX), lax.rem(s, NX)].astype(F32)
            ids, gates = tile[0:8], tile[8:16]
            marks, weights = [], []
            for o in range(4):
                eq = ids == names[o]
                marks.append(jnp.sum(jnp.where(eq, 1.0, 0.0), axis=0, keepdims=True))
                weights.append(jnp.sum(jnp.where(eq, gates, 0.0), axis=0, keepdims=True))
            pad = jnp.zeros((4, TOK), F32)
            at = pl.ds(pl.multiple_of(i * 8, 8), 8)
            asg[at, :] = jnp.concatenate(marks + [pad], axis=0)
            gts[at, :] = jnp.concatenate(weights + [pad], axis=0)
            return carry

        lax.fori_loop(0, NS, assign, 0)
        before = (
            lax.broadcasted_iota(jnp.int32, (TOK, TOK), 0)
            < lax.broadcasted_iota(jnp.int32, (TOK, TOK), 1)
        )
        upper = jnp.where(before, 1.0, 0.0).astype(BF16)
        rows = pl.ds(rel * NS * 8, NS * 8)
        marks = asg[rows, :]
        places = jnp.dot(marks.astype(BF16), upper, preferred_element_type=F32)
        code[rows, :] = jnp.where(marks > 0.5, places, -1.0)
        if rel == 1:
            return
        slot = lax.broadcasted_iota(jnp.int32, (CAP, TOK), 0).astype(F32)

        def choose(s, carry):
            rows = code[pl.ds(pl.multiple_of(s * 8, 8), 8), :]
            hot = jnp.concatenate(
                [
                    jnp.where(jnp.broadcast_to(rows[o:o + 1], (CAP, TOK)) == slot, 1.0, 0.0)
                    for o in range(4)
                ],
                axis=0,
            )
            sel[s] = hot.astype(BF16)
            selt[s] = hot.T.astype(BF16)
            return carry

        lax.fori_loop(0, NS, choose, 0)

    def build_gates():
        slot = lax.broadcasted_iota(jnp.int32, (CAP, TOK), 0).astype(F32)

        def weigh(i, carry):
            rel = lax.div(i, NS)
            s = lax.rem(i, NS)
            at = pl.ds(pl.multiple_of(i * 8, 8), 8)
            rows, weights = code[at, :], gts[at, :]
            for o in range(2):
                mine = jnp.where(
                    jnp.broadcast_to(rows[o:o + 1], (CAP, TOK)) == slot,
                    jnp.broadcast_to(weights[o:o + 1], (CAP, TOK)),
                    0.0,
                )
                total = jnp.sum(mine, axis=1, keepdims=True)
                gc[o, rel, pl.ds(pl.multiple_of(s * CAP, CAP), CAP), :] = jnp.broadcast_to(
                    total, (CAP, TOK)
                )
            return carry

        lax.fori_loop(0, 2 * NS, weigh, 0)

    def compact(n):
        def one(ys, carry):
            for xs in range(NX):
                s = ys * NX + xs
                rows = jnp.dot(sel[s], ag[n, ys, xs], preferred_element_type=F32).astype(BF16)
                zc[n, 0, 0, s] = rows[0:32]
                zc[n, 0, 1, s] = rows[32:64]
                st[n, 0, s] = rows[64:96]
                st[n, 1, s] = rows[96:128]
            return carry

        lax.fori_loop(0, NY, one, 0)

    def turn(n, rel):
        for e in (0, 1):
            zct[e, cols(n), pl.ds(rel * ROWS, ROWS)] = zc[n, rel, e].reshape(ROWS, CQ).T

    def compute_h(n):
        compact(n)
        d2_msg(n).start()
        turn(n, 0)

        def other():
            d2_msg(n - 1).wait_recv()
            turn(n - 1, 1)

        when(n >= 1, other)

    def compute_upper(q):
        def one(i, carry):
            e, rel = lax.div(i, 2), lax.rem(i, 2)
            rows = jnp.concatenate(
                [zc[n, rel, e].reshape(ROWS, CQ) for n in range(NQ)], axis=1
            )
            gs[q, e, pl.ds(pl.multiple_of(rel * ROWS, ROWS), ROWS), :] = jnp.dot(
                rows, core[e, :, cols(q)], preferred_element_type=F32
            )
            return carry

        lax.fori_loop(0, 4, one, 0)

    def gather_r(q):
        ag_done(NQ + q)
        compact(NQ + q)
        d2_msg(NQ + q).start()

    def lower_r(q, rel):
        n = NQ + q
        step = 64
        if rel == 1:
            d2_msg(n).wait_recv()

        def lower(i, carry):
            for e in (0, 1):
                at = pl.ds(pl.multiple_of(rel * ROWS + i * step, step), step)
                up = gs[q, e, at, :]
                r = zc[n, rel, e, pl.ds(i * 2, 2)].reshape(step, CQ).astype(F32)
                g = gc[e, rel, pl.ds(pl.multiple_of(i * step, step), step), :]
                g = jnp.concatenate([g, g], axis=1)
                sig = jax.nn.sigmoid(up)
                slope = sig * (1.0 + up * (1.0 - sig))
                lw[q, e, at, :] = (r * g * slope).astype(BF16)
            return carry

        lax.fori_loop(0, ROWS // step, lower, 0)

    def form_term(q):
        def term(i, carry):
            e, m = lax.div(i, 2), lax.rem(i, 2)
            at = pl.ds(pl.multiple_of(m * 512, 512), 512)
            gs[q, e, at, :] = jnp.dot(zct[e, at, :], lw[q, e], preferred_element_type=F32)
            return carry

        lax.fori_loop(0, 4, term, 0)

    def z_msg(q, k, s):
        i = 0 if s > 0 else 1
        src, dst = {
            1: (zs1, z1), 2: (z2p, z2), 3: (z2, z3), 4: (z3, z4),
        }[k]
        j = (k - 1) * 2 + i
        return rcopy(src.at[q, i], dst.at[q, i], z_s.at[q, j], z_r.at[q, j], to_z(s))

    def part_of(d):
        return pl.ds(pl.multiple_of(d * TOK, TOK), TOK)

    def z_step(k, q):
        if k == 5:
            total = gs[q, :, part_of(z), :]
            for i, s in ((0, 1), (1, -1)):
                z_msg(q, 4, s).wait_recv()
                total = total + z4[q, i].astype(F32)
            cg_ref[:, :, cols(q)] = total
            return
        for i, s in ((0, 1), (1, -1)):
            if k == 1:
                zs1[q, i] = gs[q, i, part_of(wz(z + 4)), :].astype(BF16)
            elif k == 2:
                z_msg(q, 1, s).wait_recv()
                at = part_of(wz(z + 3 * s))
                z2p[q, i, i] = (gs[q, i, at, :] + z1[q, i].astype(F32)).astype(BF16)
                z2p[q, i, 1 - i] = gs[q, 1 - i, at, :].astype(BF16)
            else:
                got = z2 if k == 3 else z3
                z_msg(q, k - 1, s).wait_recv()
                at = part_of(wz(z + (5 - k) * s))
                got[q, i] = (gs[q, :, at, :] + got[q, i].astype(F32)).astype(BF16)
            z_msg(q, k, s).start()

    def form_back(b, rel):
        def back(e, carry):
            rows = jnp.concatenate(
                [lw[q, e, pl.ds(rel * ROWS, ROWS), :] for q in range(NQ)], axis=1
            )
            total = lax.dot_general(
                rows, core[e, cols(b), :], (((1,), (1,)), ((), ())),
                preferred_element_type=F32,
            )
            rows = total.astype(BF16).reshape(NS, CAP, CQ)
            if rel == 1:
                st[b, e] = rows
            else:
                bk[b, e] = rows
            return carry

        lax.fori_loop(0, 2, back, 0)
        if rel == 1:
            d2_back(b).start()

    def scatter_b(b):
        d2_back(b).wait_recv()

        def scatter(ys, carry):
            for xs in range(NX):
                s = ys * NX + xs
                rows = bk[b, :, s].reshape(4 * CAP, CQ)
                ag[b, ys, xs] = jnp.dot(selt[s], rows, preferred_element_type=F32).astype(BF16)
            return carry

        lax.fori_loop(0, NY, scatter, 0)

    def rs_msg(b, k, half, s):
        i = 0 if s > 0 else 1
        o = half * 64
        whole = pl.ds(o, 64)
        part = pl.ds(o + 32 * i, 32)
        if k == 1:
            src = ag.at[b, wx(y + 2), :, part] if half == 0 else ag.at[b, :, wx(x + 2), part]
            dst = rs1
        else:
            src = ag.at[b, wx(y + s), :, whole] if half == 0 else ag.at[b, :, wx(x + s), whole]
            dst = rs2
        j = (k - 1) * 4 + half * 2 + i
        return rcopy(
            src, dst.at[b, half, i], rs_s.at[b, j], rs_r.at[b, j], to_y(s) if half == 0 else to_x(s)
        )

    def last_msg(b, half, j):
        whole = pl.ds(half * 64, 64)
        s = HOPS[j]
        src = ag.at[b, y, wx(x + s), whole] if half == 0 else ag.at[b, wx(y + s), x, whole]
        k = 8 + half * 3 + j
        return rcopy(
            src, rs3.at[b, half, j], rs_s.at[b, k], rs_r.at[b, k], to_x(s) if half == 0 else to_y(s)
        )

    def rs_step(k, b):
        for half in (0, 1):
            o = half * 64
            whole = pl.ds(o, 64)
            if k == 1:
                for s in (1, -1):
                    rs_msg(b, 1, half, s).start()
            elif k == 2:
                for i, s in ((0, 1), (1, -1)):
                    rs_msg(b, 1, half, s).wait_recv()
                    part = pl.ds(o + 32 * i, 32)

                    def add(j, carry):
                        yy, xx = (wx(y + s), j) if half == 0 else (j, wx(x + s))
                        ag[b, yy, xx, part] = (
                            ag[b, yy, xx, part].astype(F32) + rs1[b, half, i, j].astype(F32)
                        ).astype(BF16)
                        return carry

                    lax.fori_loop(0, 4, add, 0)
                    rs_msg(b, 2, half, s).start()
            elif k == 3:
                for s in (1, -1):
                    rs_msg(b, 2, half, s).wait_recv()

                def merge(j, carry):
                    yy, xx = (y, j) if half == 0 else (j, x)
                    ag[b, yy, xx, whole] = (
                        ag[b, yy, xx, whole].astype(F32)
                        + rs2[b, half, 0, j].astype(F32)
                        + rs2[b, half, 1, j].astype(F32)
                    ).astype(BF16)
                    return carry

                lax.fori_loop(0, 4, merge, 0)
                for j in range(3):
                    last_msg(b, half, j).start()
            else:
                total = ag[b, y, x, whole].astype(F32)
                for j in range(3):
                    last_msg(b, half, j).wait_recv()
                    total = total + rs3[b, half, j].astype(F32)
                rig_ref[whole, cols(b)] = total.astype(BF16)

    near(0, "start")
    for k in range(3):
        mt_msg(k).start()
    near(1, "start")
    for n in range(NQ):
        ag[NQ + n, y, x] = r_ref[:, n * CQ:(n + 1) * CQ]
    for k in range(3):
        mt_msg(k).wait_recv()
    for k in range(3, 6):
        mt_msg(k).start()
    near(0, "wait_recv")
    ag_own(0)
    near(1, "wait_recv")
    ag_own(1)
    for k in range(3, 6):
        mt_msg(k).wait_recv()
    mt_msg(6).start()
    build_slots(0)
    core_copy.wait()
    ag_on(0)
    ag_own(2)
    near(2, "start")

    def h_tick(n, carry):
        ag_on(n)
        when(n == 2, lambda: near(2, "wait_recv"))
        ag_own(n + 2)
        ag_done(n - 1)
        compute_h(n - 1)
        return carry

    lax.fori_loop(1, NQ + 1, h_tick, 0)
    mt_msg(6).wait_recv()
    build_slots(1)
    build_gates()
    d2_msg(NQ - 1).wait_recv()
    turn(NQ - 1, 1)

    def sent(n, carry):
        for kind in range(2):
            for half, s in SIDES:
                ag_msg(n, kind, half, s).wait_send()
        d2_msg(n).wait_send()
        return carry

    steps = {
        "o": ag_on,
        "u": compute_upper,
        "c": gather_r,
        "k": lambda q: lower_r(q, 0),
        "l": lambda q: lower_r(q, 1),
        "t": form_term,
        "b": lambda b: form_back(b, 1),
        "a": lambda b: form_back(b, 0),
        "s": scatter_b,
    }
    cleared = False
    for name, i in ORDER:
        if name == "b" and not cleared:
            lax.fori_loop(0, NQ, sent, 0)
            near(0, "wait_send")
            near(1, "wait_send")
            cleared = True
        if name[0] == "z":
            z_step(int(name[1]), i)
        elif name[0] == "r":
            rs_step(int(name[1]), i)
        else:
            steps[name](i)
        if name == "o" and i == NQ + 1:
            ag_own(2 * NQ - 1)
    lax.fori_loop(NQ, 2 * NQ, sent, 0)
    near(2, "wait_send")

    for k in range(7):
        mt_msg(k).wait_send()

    def flushed(q, carry):
        d2_back(q).wait_send()
        for k in range(1, 5):
            for s in (1, -1):
                z_msg(q, k, s).wait_send()
        for half, s in SIDES:
            for k in (1, 2):
                rs_msg(q, k, half, s).wait_send()
        for half in (0, 1):
            for j in range(3):
                last_msg(q, half, j).wait_send()
        return carry

    lax.fori_loop(0, NQ, flushed, 0)


def local(hidden_in, rank_grad, gates, expert_ids, cores):
    vmem = pl.BlockSpec(memory_space=pltpu.VMEM)
    dma = pltpu.SemaphoreType.DMA
    rig, cg = pl.pallas_call(
        body,
        out_shape=(
            jax.ShapeDtypeStruct((TOK, NQ * CQ), BF16),
            jax.ShapeDtypeStruct((2, TOK, NQ * CQ), F32),
        ),
        in_specs=[vmem, vmem, vmem, vmem, pl.BlockSpec(memory_space=pl.ANY)],
        out_specs=(vmem, vmem),
        scratch_shapes=[
            pltpu.VMEM((2 * NQ, NY, NX, TOK, CQ), BF16),
            pltpu.VMEM((2, NY, NX, 16, TOK), BF16),
            pltpu.VMEM((2, NQ * CQ, NQ * CQ), BF16),
            pltpu.VMEM((2 * NQ, 2, 2, NS, CAP, CQ), BF16),
            pltpu.VMEM((2 * NQ, 2, NS, CAP, CQ), BF16),
            pltpu.VMEM((NQ, 2, 2 * ROWS, CQ), F32),
            pltpu.VMEM((NQ, 2, 2 * ROWS, CQ), BF16),
            pltpu.VMEM((2, NQ * CQ, 2 * ROWS), BF16),
            pltpu.VMEM((NQ, 4, NS, CAP, CQ), BF16),
            pltpu.VMEM((NS, 4 * CAP, TOK), BF16),
            pltpu.VMEM((NS, TOK, 4 * CAP), BF16),
            pltpu.VMEM((2, 2, ROWS, TOK), F32),
            pltpu.VMEM((2 * NS * 8, TOK), F32),
            pltpu.VMEM((2 * NS * 8, TOK), F32),
            pltpu.VMEM((2 * NS * 8, TOK), F32),
            pltpu.VMEM((NQ, 2, TOK, CQ), BF16),
            pltpu.VMEM((NQ, 2, TOK, CQ), BF16),
            pltpu.VMEM((NQ, 2, 2, TOK, CQ), BF16),
            pltpu.VMEM((NQ, 2, 2, TOK, CQ), BF16),
            pltpu.VMEM((NQ, 2, 2, TOK, CQ), BF16),
            pltpu.VMEM((NQ, 2, 2, TOK, CQ), BF16),
            pltpu.VMEM((NQ, 2, 2, 4, 32, CQ), BF16),
            pltpu.VMEM((NQ, 2, 2, 4, 64, CQ), BF16),
            pltpu.VMEM((NQ, 2, 3, 64, CQ), BF16),
            dma, dma((3, 6)), dma((3, 6)), dma((2 * NQ, 8)), dma((2 * NQ, 8)), dma((7,)), dma((7,)),
            dma((3 * NQ,)), dma((3 * NQ,)), dma((NQ, 8)), dma((NQ, 8)),
            dma((NQ, 14)), dma((NQ, 14)),
        ],
        compiler_params=pltpu.CompilerParams(
            collective_id=0, has_side_effects=True, vmem_limit_bytes=62 * 1024 * 1024
        ),
        cost_estimate=pl.CostEstimate(
            flops=14_000_000_000, bytes_accessed=8_000_000, transcendentals=2_000_000
        ),
        name="moe_core_backward",
    )(hidden_in, rank_grad, expert_ids.T, gates.T, cores)
    return rig, jnp.transpose(cg, (1, 0, 2))


def solution(mesh):
    in_specs = (
        P(("dp", "expert"), None),
        P(("dp", "expert"), None),
        P(("dp", "expert"), None),
        P(("dp", "expert"), None),
        P("expert", None, None),
    )
    out_specs = (P(("dp", "expert"), None), P("dp", "expert", None))
    return jax.shard_map(local, mesh=mesh, in_specs=in_specs, out_specs=out_specs, check_vma=False)
```

```python
import jax
import jax.numpy as jnp
from jax import lax
from jax.experimental import pallas as pl
from jax.experimental.pallas import tpu as pltpu
from jax.sharding import PartitionSpec as P

MESH = pl.DeviceIdType.MESH
F32 = jnp.float32
BF16 = jnp.bfloat16
NZ, NY, NX = 8, 4, 4
CQ = 256
NQ = 4
TOK = 128
CAP = 32
NS = NY * NX
ROWS = NS * CAP


ORDER = (
    ("o", 5), ("u", 0), ("c", 0), ("u", 1), ("o", 6), ("k", 0), ("c", 1), ("l", 0), ("t", 0),
    ("z1", 0), ("k", 1), ("l", 1), ("t", 1), ("z1", 1), ("c", 2), ("o", 7), ("z2", 0), ("u", 2),
    ("k", 2), ("l", 2), ("z2", 1), ("u", 3), ("c", 3), ("t", 2), ("z1", 2), ("z3", 0), ("k", 3),
    ("l", 3), ("b", 0), ("t", 3), ("z1", 3), ("a", 0), ("s", 0), ("r1", 0), ("z2", 2), ("b", 1),
    ("z4", 0), ("a", 1), ("b", 2), ("z2", 3), ("r2", 0), ("a", 2), ("b", 3), ("s", 2),
    ("r1", 2), ("z3", 2), ("s", 1), ("r1", 1), ("a", 3), ("s", 3), ("r1", 3), ("r3", 0),
    ("z5", 0), ("z3", 1), ("r2", 2), ("z3", 3), ("r2", 1), ("r2", 3), ("z4", 2), ("r4", 0),
    ("z4", 1), ("r3", 2), ("z4", 3), ("r3", 1), ("z5", 2), ("r3", 3), ("r4", 2), ("z5", 1),
    ("r4", 1), ("r4", 3), ("z5", 3),
)


def when(cond, fn):
    if isinstance(cond, bool):
        if cond:
            fn()
    else:
        pl.when(cond)(fn)


def cols(i):
    if isinstance(i, int):
        return pl.ds(i * CQ, CQ)
    return pl.ds(pl.multiple_of(i * CQ, CQ), CQ)


def body(
    h_ref, r_ref, ids_ref, gates_ref, cores_ref,
    rig_ref, cg_ref,
    ag, mb, core, zc, st, gs, lw, zct, bk, sel, selt, gc, asg, code, gts,
    z1, zs1, z2p, z2, z3, z4, rs1, rs2, rs3,
    rigv, cgv, own_sem, out_sem, core_sem, p1_s, p1_r, ag_s, ag_r, mt_s, mt_r, d2_s, d2_r, z_s, z_r, rs_s, rs_r,
):
    z = lax.axis_index("dp")
    ei = lax.axis_index("expert")
    c = lax.rem(ei, 2)
    x = lax.rem(lax.div(ei, 2), NX)
    y = lax.div(ei, 2 * NX)

    def wx(v):
        return lax.rem(v + NX, NX)

    def wz(v):
        return lax.rem(v + NZ, NZ)

    def dev(zz, yy, xx, cc):
        return (zz, (yy * NX + xx) * 2 + cc)

    def to_x(s):
        return dev(z, y, wx(x + s), c)

    def to_y(s):
        return dev(z, wx(y + s), x, c)

    def to_z(s):
        return dev(wz(z + s), y, x, c)

    twin = dev(z, y, x, 1 - c)

    def rcopy(src, dst, ssem, rsem, device):
        return pltpu.make_async_remote_copy(
            src_ref=src, dst_ref=dst, send_sem=ssem, recv_sem=rsem,
            device_id=device, device_id_type=MESH,
        )

    barrier = pltpu.get_barrier_semaphore()
    for device in (
        twin, to_x(1), to_x(-1), to_x(2), to_y(1), to_y(-1), to_y(2), to_z(1), to_z(-1)
    ):
        pl.semaphore_signal(barrier, inc=1, device_id=device, device_id_type=MESH)

    def own_copy(n):
        src = h_ref if n < NQ else r_ref
        return pltpu.make_async_copy(src.at[:, cols(n % NQ)], ag.at[n, y, x], own_sem.at[n])

    for n in range(NQ):
        own_copy(n).start()
    core_copy = pltpu.make_async_copy(cores_ref, core, core_sem)
    core_copy.start()
    for n in range(NQ, 2 * NQ):
        own_copy(n).start()
    mb[0, y, x] = jnp.concatenate(
        [ids_ref[...].astype(F32), gates_ref[...].astype(F32)], axis=0
    ).astype(BF16)
    pl.semaphore_wait(barrier, 9)

    SIDES = ((0, 1), (0, -1), (1, 1), (1, -1))
    HOPS = (1, -1, 2)
    GROUPS = ((0, 1), (1, NQ - 1), (NQ, NQ))

    def near_msg(g, half, j):
        lo, count = GROUPS[g]
        ref = ag.at[pl.ds(lo, count), y, x, pl.ds(half * 64, 64)]
        k = half * 3 + j
        device = to_x(HOPS[j]) if half == 0 else to_y(HOPS[j])
        return rcopy(ref, ref, p1_s.at[g, k], p1_r.at[g, k], device)

    def near(g, act):
        for half in (0, 1):
            for j in range(3):
                getattr(near_msg(g, half, j), act)()

    def ag_msg(n, kind, half, s):
        o = half * 64
        whole = pl.ds(o, 64)
        part = pl.ds(o + (0 if s > 0 else 32), 32)
        if kind == 0:
            ref = ag.at[n, y, :, whole] if half == 0 else ag.at[n, :, x, whole]
        else:
            ref = ag.at[n, wx(y - s), :, part] if half == 0 else ag.at[n, :, wx(x - s), part]
        k = kind * 4 + half * 2 + (0 if s > 0 else 1)
        return rcopy(
            ref, ref, ag_s.at[n, k], ag_r.at[n, k], to_y(s) if half == 0 else to_x(s)
        )

    def ag_own(n):
        for half, s in SIDES:
            ag_msg(n, 0, half, s).start()

    def ag_on(n):
        for half, s in SIDES:
            ag_msg(n, 0, half, s).wait_recv()
            ag_msg(n, 1, half, s).start()

    def ag_done(n):
        for half, s in SIDES:
            ag_msg(n, 1, half, s).wait_recv()

    def mt_msg(k):
        if k < 3:
            ref, device = mb.at[0, y, x], to_x(HOPS[k])
        elif k < 6:
            ref, device = mb.at[0, y], to_y(HOPS[k - 3])
        else:
            return rcopy(mb.at[0], mb.at[1], mt_s.at[k], mt_r.at[k], twin)
        return rcopy(ref, ref, mt_s.at[k], mt_r.at[k], device)

    def d2_msg(n):
        return rcopy(st.at[n], zc.at[n, 1], d2_s.at[n], d2_r.at[n], twin)

    def d2_back(b):
        k = 2 * NQ + b
        return rcopy(st.at[b], bk.at[b, pl.ds(2, 2)], d2_s.at[k], d2_r.at[k], twin)

    def build_slots(rel):
        first = (y * NX + x) * 4
        names = []
        for o in range(4):
            e = first + 2 * c + o if o < 2 else first + 2 * (1 - c) + (o - 2)
            names.append(e.astype(F32))

        def assign(s, carry):
            i = rel * NS + s
            tile = mb[rel, lax.div(s, NX), lax.rem(s, NX)].astype(F32)
            ids, gates = tile[0:8], tile[8:16]
            marks, weights = [], []
            for o in range(4):
                eq = ids == names[o]
                marks.append(jnp.sum(jnp.where(eq, 1.0, 0.0), axis=0, keepdims=True))
                weights.append(jnp.sum(jnp.where(eq, gates, 0.0), axis=0, keepdims=True))
            pad = jnp.zeros((4, TOK), F32)
            at = pl.ds(pl.multiple_of(i * 8, 8), 8)
            asg[at, :] = jnp.concatenate(marks + [pad], axis=0)
            gts[at, :] = jnp.concatenate(weights + [pad], axis=0)
            return carry

        lax.fori_loop(0, NS, assign, 0)
        before = (
            lax.broadcasted_iota(jnp.int32, (TOK, TOK), 0)
            < lax.broadcasted_iota(jnp.int32, (TOK, TOK), 1)
        )
        upper = jnp.where(before, 1.0, 0.0).astype(BF16)
        rows = pl.ds(rel * NS * 8, NS * 8)
        marks = asg[rows, :]
        places = jnp.dot(marks.astype(BF16), upper, preferred_element_type=F32)
        code[rows, :] = jnp.where(marks > 0.5, places, -1.0)
        if rel == 1:
            return
        slot = lax.broadcasted_iota(jnp.int32, (CAP, TOK), 0).astype(F32)

        def choose(s, carry):
            rows = code[pl.ds(pl.multiple_of(s * 8, 8), 8), :]
            hot = jnp.concatenate(
                [
                    jnp.where(jnp.broadcast_to(rows[o:o + 1], (CAP, TOK)) == slot, 1.0, 0.0)
                    for o in range(4)
                ],
                axis=0,
            )
            sel[s] = hot.astype(BF16)
            selt[s] = hot.T.astype(BF16)
            return carry

        lax.fori_loop(0, NS, choose, 0)

    def build_gates():
        slot = lax.broadcasted_iota(jnp.int32, (CAP, TOK), 0).astype(F32)

        def weigh(i, carry):
            rel = lax.div(i, NS)
            s = lax.rem(i, NS)
            at = pl.ds(pl.multiple_of(i * 8, 8), 8)
            rows, weights = code[at, :], gts[at, :]
            for o in range(2):
                mine = jnp.where(
                    jnp.broadcast_to(rows[o:o + 1], (CAP, TOK)) == slot,
                    jnp.broadcast_to(weights[o:o + 1], (CAP, TOK)),
                    0.0,
                )
                total = jnp.sum(mine, axis=1, keepdims=True)
                gc[o, rel, pl.ds(pl.multiple_of(s * CAP, CAP), CAP), :] = jnp.broadcast_to(
                    total, (CAP, TOK)
                )
            return carry

        lax.fori_loop(0, 2 * NS, weigh, 0)

    def compact(n):
        for s in range(NS):
            rows = jnp.dot(
                sel[s], ag[n, s // NX, s % NX], preferred_element_type=F32
            ).astype(BF16)
            zc[n, 0, 0, s] = rows[0:32]
            zc[n, 0, 1, s] = rows[32:64]
            st[n, 0, s] = rows[64:96]
            st[n, 1, s] = rows[96:128]

    def turn(n, rel):
        for e in (0, 1):
            zct[e, cols(n), pl.ds(rel * ROWS, ROWS)] = zc[n, rel, e].reshape(ROWS, CQ).T

    def compute_h(n):
        compact(n)
        d2_msg(n).start()
        turn(n, 0)

        def other():
            d2_msg(n - 1).wait_recv()
            turn(n - 1, 1)

        when(n >= 1, other)

    def compute_upper(q):
        for e in (0, 1):
            for rel in (0, 1):
                rows = jnp.concatenate(
                    [zc[n, rel, e].reshape(ROWS, CQ) for n in range(NQ)], axis=1
                )
                gs[q, e, pl.ds(rel * ROWS, ROWS), :] = jnp.dot(
                    rows, core[e, :, cols(q)], preferred_element_type=F32
                )

    def gather_r(q):
        ag_done(NQ + q)
        compact(NQ + q)
        d2_msg(NQ + q).start()

    def lower_r(q, rel):
        n = NQ + q
        step = 64
        if rel == 1:
            d2_msg(n).wait_recv()

        def lower(i, carry):
            for e in (0, 1):
                at = pl.ds(pl.multiple_of(rel * ROWS + i * step, step), step)
                up = gs[q, e, at, :]
                r = zc[n, rel, e, pl.ds(i * 2, 2)].reshape(step, CQ).astype(F32)
                g = gc[e, rel, pl.ds(pl.multiple_of(i * step, step), step), :]
                g = jnp.concatenate([g, g], axis=1)
                sig = jax.nn.sigmoid(up)
                slope = sig * (1.0 + up * (1.0 - sig))
                lw[q, e, at, :] = (r * g * slope).astype(BF16)
            return carry

        lax.fori_loop(0, ROWS // step, lower, 0)

    def form_term(q):
        for e in (0, 1):
            for m in (0, 1):
                at = pl.ds(m * 512, 512)
                gs[q, e, at, :] = jnp.dot(zct[e, at, :], lw[q, e], preferred_element_type=F32)

    def z_msg(q, k, s):
        i = 0 if s > 0 else 1
        src, dst = {
            1: (zs1, z1), 2: (z2p, z2), 3: (z2, z3), 4: (z3, z4),
        }[k]
        j = (k - 1) * 2 + i
        return rcopy(src.at[q, i], dst.at[q, i], z_s.at[q, j], z_r.at[q, j], to_z(s))

    def out_copy(which, i):
        if which:
            return pltpu.make_async_copy(cgv.at[i], cg_ref.at[:, :, cols(i)], out_sem.at[1, i])
        return pltpu.make_async_copy(rigv.at[i], rig_ref.at[:, cols(i)], out_sem.at[0, i])

    def part_of(d):
        return pl.ds(pl.multiple_of(d * TOK, TOK), TOK)

    def z_step(k, q):
        if k == 5:
            total = gs[q, :, part_of(z), :]
            for i, s in ((0, 1), (1, -1)):
                z_msg(q, 4, s).wait_recv()
                total = total + z4[q, i].astype(F32)
            cgv[q] = total
            out_copy(1, q).start()
            return
        for i, s in ((0, 1), (1, -1)):
            if k == 1:
                zs1[q, i] = gs[q, i, part_of(wz(z + 4)), :].astype(BF16)
            elif k == 2:
                z_msg(q, 1, s).wait_recv()
                at = part_of(wz(z + 3 * s))
                z2p[q, i, i] = (gs[q, i, at, :] + z1[q, i].astype(F32)).astype(BF16)
                z2p[q, i, 1 - i] = gs[q, 1 - i, at, :].astype(BF16)
            else:
                got = z2 if k == 3 else z3
                z_msg(q, k - 1, s).wait_recv()
                at = part_of(wz(z + (5 - k) * s))
                got[q, i] = (gs[q, :, at, :] + got[q, i].astype(F32)).astype(BF16)
            z_msg(q, k, s).start()

    def form_back(b, rel):
        for e in (0, 1):
            rows = jnp.concatenate(
                [lw[q, e, pl.ds(rel * ROWS, ROWS), :] for q in range(NQ)], axis=1
            )
            total = lax.dot_general(
                rows, core[e, cols(b), :], (((1,), (1,)), ((), ())),
                preferred_element_type=F32,
            )
            rows = total.astype(BF16).reshape(NS, CAP, CQ)
            if rel == 1:
                st[b, e] = rows
            else:
                bk[b, e] = rows
        if rel == 1:
            d2_back(b).start()

    def scatter_b(b):
        d2_back(b).wait_recv()

        for s in range(NS):
            rows = bk[b, :, s].reshape(4 * CAP, CQ)
            ag[b, s // NX, s % NX] = jnp.dot(
                selt[s], rows, preferred_element_type=F32
            ).astype(BF16)

    def rs_msg(b, k, half, s):
        i = 0 if s > 0 else 1
        o = half * 64
        whole = pl.ds(o, 64)
        part = pl.ds(o + 32 * i, 32)
        if k == 1:
            src = ag.at[b, wx(y + 2), :, part] if half == 0 else ag.at[b, :, wx(x + 2), part]
            dst = rs1
        else:
            src = ag.at[b, wx(y + s), :, whole] if half == 0 else ag.at[b, :, wx(x + s), whole]
            dst = rs2
        j = (k - 1) * 4 + half * 2 + i
        return rcopy(
            src, dst.at[b, half, i], rs_s.at[b, j], rs_r.at[b, j], to_y(s) if half == 0 else to_x(s)
        )

    def last_msg(b, half, j):
        whole = pl.ds(half * 64, 64)
        s = HOPS[j]
        src = ag.at[b, y, wx(x + s), whole] if half == 0 else ag.at[b, wx(y + s), x, whole]
        k = 8 + half * 3 + j
        return rcopy(
            src, rs3.at[b, half, j], rs_s.at[b, k], rs_r.at[b, k], to_x(s) if half == 0 else to_y(s)
        )

    def rs_step(k, b):
        for half in (0, 1):
            o = half * 64
            whole = pl.ds(o, 64)
            if k == 1:
                for s in (1, -1):
                    rs_msg(b, 1, half, s).start()
            elif k == 2:
                for i, s in ((0, 1), (1, -1)):
                    rs_msg(b, 1, half, s).wait_recv()
                    part = pl.ds(o + 32 * i, 32)

                    def add(j, carry):
                        yy, xx = (wx(y + s), j) if half == 0 else (j, wx(x + s))
                        ag[b, yy, xx, part] = (
                            ag[b, yy, xx, part].astype(F32) + rs1[b, half, i, j].astype(F32)
                        ).astype(BF16)
                        return carry

                    lax.fori_loop(0, 4, add, 0)
                    rs_msg(b, 2, half, s).start()
            elif k == 3:
                for s in (1, -1):
                    rs_msg(b, 2, half, s).wait_recv()

                def merge(j, carry):
                    yy, xx = (y, j) if half == 0 else (j, x)
                    ag[b, yy, xx, whole] = (
                        ag[b, yy, xx, whole].astype(F32)
                        + rs2[b, half, 0, j].astype(F32)
                        + rs2[b, half, 1, j].astype(F32)
                    ).astype(BF16)
                    return carry

                lax.fori_loop(0, 4, merge, 0)
                for j in range(3):
                    last_msg(b, half, j).start()
            elif k == 4:
                total = ag[b, y, x, whole].astype(F32)
                for j in range(3):
                    last_msg(b, half, j).wait_recv()
                    total = total + rs3[b, half, j].astype(F32)
                rigv[b, whole] = total.astype(BF16)
        if k == 4:
            out_copy(0, b).start()

    own_copy(0).wait()
    near(0, "start")
    for k in range(3):
        mt_msg(k).start()
    for n in range(1, NQ):
        own_copy(n).wait()
    near(1, "start")
    for k in range(3):
        mt_msg(k).wait_recv()
    for k in range(3, 6):
        mt_msg(k).start()
    near(0, "wait_recv")
    ag_own(0)
    near(1, "wait_recv")
    ag_own(1)
    for k in range(3, 6):
        mt_msg(k).wait_recv()
    mt_msg(6).start()
    build_slots(0)
    core_copy.wait()
    ag_on(0)
    ag_own(2)
    for n in range(NQ, 2 * NQ):
        own_copy(n).wait()
    near(2, "start")

    def h_tick(n, carry):
        ag_on(n)
        when(n == 2, lambda: near(2, "wait_recv"))
        ag_own(n + 2)
        ag_done(n - 1)
        compute_h(n - 1)
        return carry

    lax.fori_loop(1, NQ + 1, h_tick, 0)
    mt_msg(6).wait_recv()
    build_slots(1)
    build_gates()
    d2_msg(NQ - 1).wait_recv()
    turn(NQ - 1, 1)

    def sent(n, carry):
        for kind in range(2):
            for half, s in SIDES:
                ag_msg(n, kind, half, s).wait_send()
        d2_msg(n).wait_send()
        return carry

    steps = {
        "o": ag_on,
        "u": compute_upper,
        "c": gather_r,
        "k": lambda q: lower_r(q, 0),
        "l": lambda q: lower_r(q, 1),
        "t": form_term,
        "b": lambda b: form_back(b, 1),
        "a": lambda b: form_back(b, 0),
        "s": scatter_b,
    }
    cleared = False
    for name, i in ORDER:
        if name == "b" and not cleared:
            lax.fori_loop(0, NQ, sent, 0)
            near(0, "wait_send")
            near(1, "wait_send")
            cleared = True
        if name[0] == "z":
            z_step(int(name[1]), i)
        elif name[0] == "r":
            rs_step(int(name[1]), i)
        else:
            steps[name](i)
        if name == "o" and i == NQ + 1:
            ag_own(2 * NQ - 1)
    lax.fori_loop(NQ, 2 * NQ, sent, 0)
    near(2, "wait_send")

    for k in range(7):
        mt_msg(k).wait_send()

    def flushed(q, carry):
        d2_back(q).wait_send()
        for k in range(1, 5):
            for s in (1, -1):
                z_msg(q, k, s).wait_send()
        for half, s in SIDES:
            for k in (1, 2):
                rs_msg(q, k, half, s).wait_send()
        for half in (0, 1):
            for j in range(3):
                last_msg(q, half, j).wait_send()
        return carry

    lax.fori_loop(0, NQ, flushed, 0)
    for which in (0, 1):
        for i in range(NQ):
            out_copy(which, i).wait()


def local(hidden_in, rank_grad, gates, expert_ids, cores):
    vmem = pl.BlockSpec(memory_space=pltpu.VMEM)
    hbm = pl.BlockSpec(memory_space=pl.ANY)
    dma = pltpu.SemaphoreType.DMA
    rig, cg = pl.pallas_call(
        body,
        out_shape=(
            jax.ShapeDtypeStruct((TOK, NQ * CQ), BF16),
            jax.ShapeDtypeStruct((2, TOK, NQ * CQ), F32),
        ),
        in_specs=[hbm, hbm, vmem, vmem, hbm],
        out_specs=(hbm, hbm),
        scratch_shapes=[
            pltpu.VMEM((2 * NQ, NY, NX, TOK, CQ), BF16),
            pltpu.VMEM((2, NY, NX, 16, TOK), BF16),
            pltpu.VMEM((2, NQ * CQ, NQ * CQ), BF16),
            pltpu.VMEM((2 * NQ, 2, 2, NS, CAP, CQ), BF16),
            pltpu.VMEM((2 * NQ, 2, NS, CAP, CQ), BF16),
            pltpu.VMEM((NQ, 2, 2 * ROWS, CQ), F32),
            pltpu.VMEM((NQ, 2, 2 * ROWS, CQ), BF16),
            pltpu.VMEM((2, NQ * CQ, 2 * ROWS), BF16),
            pltpu.VMEM((NQ, 4, NS, CAP, CQ), BF16),
            pltpu.VMEM((NS, 4 * CAP, TOK), BF16),
            pltpu.VMEM((NS, TOK, 4 * CAP), BF16),
            pltpu.VMEM((2, 2, ROWS, TOK), F32),
            pltpu.VMEM((2 * NS * 8, TOK), F32),
            pltpu.VMEM((2 * NS * 8, TOK), F32),
            pltpu.VMEM((2 * NS * 8, TOK), F32),
            pltpu.VMEM((NQ, 2, TOK, CQ), BF16),
            pltpu.VMEM((NQ, 2, TOK, CQ), BF16),
            pltpu.VMEM((NQ, 2, 2, TOK, CQ), BF16),
            pltpu.VMEM((NQ, 2, 2, TOK, CQ), BF16),
            pltpu.VMEM((NQ, 2, 2, TOK, CQ), BF16),
            pltpu.VMEM((NQ, 2, 2, TOK, CQ), BF16),
            pltpu.VMEM((NQ, 2, 2, 4, 32, CQ), BF16),
            pltpu.VMEM((NQ, 2, 2, 4, 64, CQ), BF16),
            pltpu.VMEM((NQ, 2, 3, 64, CQ), BF16),
            pltpu.VMEM((NQ, TOK, CQ), BF16),
            pltpu.VMEM((NQ, 2, TOK, CQ), F32),
            dma((2 * NQ,)), dma((2, NQ)),
            dma, dma((3, 6)), dma((3, 6)), dma((2 * NQ, 8)), dma((2 * NQ, 8)), dma((7,)), dma((7,)),
            dma((3 * NQ,)), dma((3 * NQ,)), dma((NQ, 8)), dma((NQ, 8)),
            dma((NQ, 14)), dma((NQ, 14)),
        ],
        compiler_params=pltpu.CompilerParams(
            collective_id=0, has_side_effects=True, vmem_limit_bytes=62 * 1024 * 1024
        ),
        cost_estimate=pl.CostEstimate(
            flops=14_000_000_000, bytes_accessed=8_000_000, transcendentals=2_000_000
        ),
        name="moe_core_backward",
    )(hidden_in, rank_grad, expert_ids.T, gates.T, cores)
    return rig, jnp.transpose(cg, (1, 0, 2))


def solution(mesh):
    in_specs = (
        P(("dp", "expert"), None),
        P(("dp", "expert"), None),
        P(("dp", "expert"), None),
        P(("dp", "expert"), None),
        P("expert", None, None),
    )
    out_specs = (P(("dp", "expert"), None), P("dp", "expert", None))
    return jax.shard_map(local, mesh=mesh, in_specs=in_specs, out_specs=out_specs, check_vma=False)
```

```python
import jax
import jax.numpy as jnp
from jax import lax
from jax.experimental import pallas as pl
from jax.experimental.pallas import tpu as pltpu
from jax.sharding import PartitionSpec as P

MESH = pl.DeviceIdType.MESH
F32 = jnp.float32
BF16 = jnp.bfloat16
NZ, NY, NX = 8, 4, 4
CQ = 256
NQ = 4
TOK = 128
CAP = 32
NS = NY * NX
ROWS = NS * CAP


ORDER = (
    ("o", 5), ("u", 0), ("c", 0), ("u", 1), ("o", 6), ("k", 0), ("c", 1), ("l", 0), ("t", 0),
    ("z1", 0), ("k", 1), ("l", 1), ("t", 1), ("z1", 1), ("c", 2), ("o", 7), ("z2", 0), ("u", 2),
    ("k", 2), ("l", 2), ("z2", 1), ("u", 3), ("c", 3), ("t", 2), ("z1", 2), ("z3", 0), ("k", 3),
    ("l", 3), ("b", 0), ("t", 3), ("z1", 3), ("a", 0), ("s", 0), ("r1", 0), ("z2", 2), ("b", 1),
    ("z4", 0), ("a", 1), ("b", 2), ("z2", 3), ("r2", 0), ("a", 2), ("b", 3), ("s", 2),
    ("r1", 2), ("z3", 2), ("s", 1), ("r1", 1), ("a", 3), ("s", 3), ("r1", 3), ("r3", 0),
    ("z5", 0), ("z3", 1), ("r2", 2), ("z3", 3), ("r2", 1), ("r2", 3), ("z4", 2), ("r4", 0),
    ("z4", 1), ("r3", 2), ("z4", 3), ("r3", 1), ("z5", 2), ("r3", 3), ("r4", 2), ("z5", 1),
    ("r4", 1), ("r4", 3), ("z5", 3),
)


def when(cond, fn):
    if isinstance(cond, bool):
        if cond:
            fn()
    else:
        pl.when(cond)(fn)


def cols(i):
    if isinstance(i, int):
        return pl.ds(i * CQ, CQ)
    return pl.ds(pl.multiple_of(i * CQ, CQ), CQ)


def body(
    h_ref, r_ref, ids_ref, gates_ref, cores_ref,
    rig_ref, cg_ref,
    ag, mb, core, zc, st, gs, lw, zct, bk, sel, selt, gc, asg, code, gts,
    z1, zs1, z2p, z2, z3, z4, rs1, rs2, rs3,
    rigv, cgv, own_sem, out_sem, core_sem, p1_s, p1_r, ag_s, ag_r, mt_s, mt_r, d2_s, d2_r, z_s, z_r, rs_s, rs_r,
):
    z = lax.axis_index("dp")
    ei = lax.axis_index("expert")
    c = lax.rem(ei, 2)
    x = lax.rem(lax.div(ei, 2), NX)
    y = lax.div(ei, 2 * NX)

    def wx(v):
        return lax.rem(v + NX, NX)

    def wz(v):
        return lax.rem(v + NZ, NZ)

    def dev(zz, yy, xx, cc):
        return (zz, (yy * NX + xx) * 2 + cc)

    def to_x(s):
        return dev(z, y, wx(x + s), c)

    def to_y(s):
        return dev(z, wx(y + s), x, c)

    def to_z(s):
        return dev(wz(z + s), y, x, c)

    twin = dev(z, y, x, 1 - c)

    def rcopy(src, dst, ssem, rsem, device):
        return pltpu.make_async_remote_copy(
            src_ref=src, dst_ref=dst, send_sem=ssem, recv_sem=rsem,
            device_id=device, device_id_type=MESH,
        )

    barrier = pltpu.get_barrier_semaphore()
    for device in (
        twin, to_x(1), to_x(-1), to_x(2), to_y(1), to_y(-1), to_y(2), to_z(1), to_z(-1)
    ):
        pl.semaphore_signal(barrier, inc=1, device_id=device, device_id_type=MESH)

    def own_copy(n):
        src = h_ref if n < NQ else r_ref
        return pltpu.make_async_copy(src.at[:, cols(n % NQ)], ag.at[n, y, x], own_sem.at[n])

    for n in range(NQ):
        own_copy(n).start()
    core_copy = pltpu.make_async_copy(cores_ref, core, core_sem)
    core_copy.start()
    for n in range(NQ, 2 * NQ):
        own_copy(n).start()
    mb[0, y, x] = jnp.concatenate(
        [ids_ref[...].astype(F32), gates_ref[...].astype(F32)], axis=0
    ).astype(BF16)
    pl.semaphore_wait(barrier, 9)

    SIDES = ((0, 1), (0, -1), (1, 1), (1, -1))
    HOPS = (1, -1, 2)
    GROUPS = ((0, 1), (1, NQ - 1), (NQ, NQ))

    RELAYED = 2

    def near_msg(g, half, j):
        lo, count = GROUPS[g]
        rounds = pl.ds(lo, count)
        o = half * 64
        if g < RELAYED:
            hop = HOPS[j]
            ref = ag.at[rounds, y, x, pl.ds(o, 64)]
        else:
            hop = HOPS[j % 2]
            if j < 2:
                ref = ag.at[rounds, y, x, pl.ds(o, 64)]
            else:
                part = pl.ds(o + 32 * (j - 2), 32)
                yy, xx = (y, wx(x - hop)) if half == 0 else (wx(y - hop), x)
                ref = ag.at[rounds, yy, xx, part]
        k = half * 4 + j
        device = to_x(hop) if half == 0 else to_y(hop)
        return rcopy(ref, ref, p1_s.at[g, k], p1_r.at[g, k], device)

    def near(g, act):
        count = 3 if g < RELAYED else 4 if act == "wait_send" else 2
        for half in (0, 1):
            for j in range(count):
                getattr(near_msg(g, half, j), act)()

    def near_on(g):
        if g >= RELAYED:
            for half in (0, 1):
                for j in (0, 1):
                    near_msg(g, half, j).wait_recv()
                    near_msg(g, half, j + 2).start()

    def near_done(g):
        if g < RELAYED:
            near(g, "wait_recv")
        else:
            for half in (0, 1):
                for j in (2, 3):
                    near_msg(g, half, j).wait_recv()

    def ag_msg(n, kind, half, s):
        o = half * 64
        whole = pl.ds(o, 64)
        part = pl.ds(o + (0 if s > 0 else 32), 32)
        if kind == 0:
            ref = ag.at[n, y, :, whole] if half == 0 else ag.at[n, :, x, whole]
        else:
            ref = ag.at[n, wx(y - s), :, part] if half == 0 else ag.at[n, :, wx(x - s), part]
        k = kind * 4 + half * 2 + (0 if s > 0 else 1)
        return rcopy(
            ref, ref, ag_s.at[n, k], ag_r.at[n, k], to_y(s) if half == 0 else to_x(s)
        )

    def ag_own(n):
        for half, s in SIDES:
            ag_msg(n, 0, half, s).start()

    def ag_on(n):
        for half, s in SIDES:
            ag_msg(n, 0, half, s).wait_recv()
            ag_msg(n, 1, half, s).start()

    def ag_done(n):
        for half, s in SIDES:
            ag_msg(n, 1, half, s).wait_recv()

    def mt_msg(k):
        if k < 3:
            ref, device = mb.at[0, y, x], to_x(HOPS[k])
        elif k < 6:
            ref, device = mb.at[0, y], to_y(HOPS[k - 3])
        else:
            return rcopy(mb.at[0], mb.at[1], mt_s.at[k], mt_r.at[k], twin)
        return rcopy(ref, ref, mt_s.at[k], mt_r.at[k], device)

    def d2_msg(n):
        return rcopy(st.at[n], zc.at[n, 1], d2_s.at[n], d2_r.at[n], twin)

    def d2_back(b):
        k = 2 * NQ + b
        return rcopy(st.at[b], bk.at[b, pl.ds(2, 2)], d2_s.at[k], d2_r.at[k], twin)

    def build_slots(rel):
        first = (y * NX + x) * 4
        names = []
        for o in range(4):
            e = first + 2 * c + o if o < 2 else first + 2 * (1 - c) + (o - 2)
            names.append(e.astype(F32))

        def assign(s, carry):
            i = rel * NS + s
            tile = mb[rel, lax.div(s, NX), lax.rem(s, NX)].astype(F32)
            ids, gates = tile[0:8], tile[8:16]
            marks, weights = [], []
            for o in range(4):
                eq = ids == names[o]
                marks.append(jnp.sum(jnp.where(eq, 1.0, 0.0), axis=0, keepdims=True))
                weights.append(jnp.sum(jnp.where(eq, gates, 0.0), axis=0, keepdims=True))
            pad = jnp.zeros((4, TOK), F32)
            at = pl.ds(pl.multiple_of(i * 8, 8), 8)
            asg[at, :] = jnp.concatenate(marks + [pad], axis=0)
            gts[at, :] = jnp.concatenate(weights + [pad], axis=0)
            return carry

        lax.fori_loop(0, NS, assign, 0)
        before = (
            lax.broadcasted_iota(jnp.int32, (TOK, TOK), 0)
            < lax.broadcasted_iota(jnp.int32, (TOK, TOK), 1)
        )
        upper = jnp.where(before, 1.0, 0.0).astype(BF16)
        rows = pl.ds(rel * NS * 8, NS * 8)
        marks = asg[rows, :]
        places = jnp.dot(marks.astype(BF16), upper, preferred_element_type=F32)
        code[rows, :] = jnp.where(marks > 0.5, places, -1.0)
        if rel == 1:
            return
        slot = lax.broadcasted_iota(jnp.int32, (CAP, TOK), 0).astype(F32)

        def choose(s, carry):
            rows = code[pl.ds(pl.multiple_of(s * 8, 8), 8), :]
            hot = jnp.concatenate(
                [
                    jnp.where(jnp.broadcast_to(rows[o:o + 1], (CAP, TOK)) == slot, 1.0, 0.0)
                    for o in range(4)
                ],
                axis=0,
            )
            sel[s] = hot.astype(BF16)
            selt[s] = hot.T.astype(BF16)
            return carry

        lax.fori_loop(0, NS, choose, 0)

    def build_gates():
        slot = lax.broadcasted_iota(jnp.int32, (CAP, TOK), 0).astype(F32)

        def weigh(i, carry):
            rel = lax.div(i, NS)
            s = lax.rem(i, NS)
            at = pl.ds(pl.multiple_of(i * 8, 8), 8)
            rows, weights = code[at, :], gts[at, :]
            for o in range(2):
                mine = jnp.where(
                    jnp.broadcast_to(rows[o:o + 1], (CAP, TOK)) == slot,
                    jnp.broadcast_to(weights[o:o + 1], (CAP, TOK)),
                    0.0,
                )
                total = jnp.sum(mine, axis=1, keepdims=True)
                gc[o, rel, pl.ds(pl.multiple_of(s * CAP, CAP), CAP), :] = jnp.broadcast_to(
                    total, (CAP, TOK)
                )
            return carry

        lax.fori_loop(0, 2 * NS, weigh, 0)

    def compact(n):
        for s in range(NS):
            rows = jnp.dot(
                sel[s], ag[n, s // NX, s % NX], preferred_element_type=F32
            ).astype(BF16)
            zc[n, 0, 0, s] = rows[0:32]
            zc[n, 0, 1, s] = rows[32:64]
            st[n, 0, s] = rows[64:96]
            st[n, 1, s] = rows[96:128]

    def turn(n, rel):
        for e in (0, 1):
            zct[e, cols(n), pl.ds(rel * ROWS, ROWS)] = zc[n, rel, e].reshape(ROWS, CQ).T

    def compute_h(n):
        compact(n)
        d2_msg(n).start()
        turn(n, 0)

        def other():
            d2_msg(n - 1).wait_recv()
            turn(n - 1, 1)

        when(n >= 1, other)

    def compute_upper(q):
        for e in (0, 1):
            for rel in (0, 1):
                rows = jnp.concatenate(
                    [zc[n, rel, e].reshape(ROWS, CQ) for n in range(NQ)], axis=1
                )
                gs[q, e, pl.ds(rel * ROWS, ROWS), :] = jnp.dot(
                    rows, core[e, :, cols(q)], preferred_element_type=F32
                )

    def gather_r(q):
        ag_done(NQ + q)
        compact(NQ + q)
        d2_msg(NQ + q).start()

    def lower_r(q, rel):
        n = NQ + q
        step = 64
        if rel == 1:
            d2_msg(n).wait_recv()

        def lower(i, carry):
            for e in (0, 1):
                at = pl.ds(pl.multiple_of(rel * ROWS + i * step, step), step)
                up = gs[q, e, at, :]
                r = zc[n, rel, e, pl.ds(i * 2, 2)].reshape(step, CQ).astype(F32)
                g = gc[e, rel, pl.ds(pl.multiple_of(i * step, step), step), :]
                g = jnp.concatenate([g, g], axis=1)
                sig = jax.nn.sigmoid(up)
                slope = sig * (1.0 + up * (1.0 - sig))
                lw[q, e, at, :] = (r * g * slope).astype(BF16)
            return carry

        lax.fori_loop(0, ROWS // step, lower, 0)

    def form_term(q):
        for e in (0, 1):
            for m in (0, 1):
                at = pl.ds(m * 512, 512)
                gs[q, e, at, :] = jnp.dot(zct[e, at, :], lw[q, e], preferred_element_type=F32)

    def z_msg(q, k, s):
        i = 0 if s > 0 else 1
        src, dst = {
            1: (zs1, z1), 2: (z2p, z2), 3: (z2, z3), 4: (z3, z4),
        }[k]
        j = (k - 1) * 2 + i
        return rcopy(src.at[q, i], dst.at[q, i], z_s.at[q, j], z_r.at[q, j], to_z(s))

    def out_copy(which, i):
        if which:
            return pltpu.make_async_copy(cgv.at[i], cg_ref.at[:, :, cols(i)], out_sem.at[1, i])
        return pltpu.make_async_copy(rigv.at[i], rig_ref.at[:, cols(i)], out_sem.at[0, i])

    def part_of(d):
        return pl.ds(pl.multiple_of(d * TOK, TOK), TOK)

    def z_step(k, q):
        if k == 5:
            total = gs[q, :, part_of(z), :]
            for i, s in ((0, 1), (1, -1)):
                z_msg(q, 4, s).wait_recv()
                total = total + z4[q, i].astype(F32)
            cgv[q] = total
            out_copy(1, q).start()
            return
        for i, s in ((0, 1), (1, -1)):
            if k == 1:
                zs1[q, i] = gs[q, i, part_of(wz(z + 4)), :].astype(BF16)
            elif k == 2:
                z_msg(q, 1, s).wait_recv()
                at = part_of(wz(z + 3 * s))
                z2p[q, i, i] = (gs[q, i, at, :] + z1[q, i].astype(F32)).astype(BF16)
                z2p[q, i, 1 - i] = gs[q, 1 - i, at, :].astype(BF16)
            else:
                got = z2 if k == 3 else z3
                z_msg(q, k - 1, s).wait_recv()
                at = part_of(wz(z + (5 - k) * s))
                got[q, i] = (gs[q, :, at, :] + got[q, i].astype(F32)).astype(BF16)
            z_msg(q, k, s).start()

    def form_back(b, rel):
        for e in (0, 1):
            rows = jnp.concatenate(
                [lw[q, e, pl.ds(rel * ROWS, ROWS), :] for q in range(NQ)], axis=1
            )
            total = lax.dot_general(
                rows, core[e, cols(b), :], (((1,), (1,)), ((), ())),
                preferred_element_type=F32,
            )
            rows = total.astype(BF16).reshape(NS, CAP, CQ)
            if rel == 1:
                st[b, e] = rows
            else:
                bk[b, e] = rows
        if rel == 1:
            d2_back(b).start()

    def scatter_b(b):
        d2_back(b).wait_recv()

        for s in range(NS):
            rows = bk[b, :, s].reshape(4 * CAP, CQ)
            ag[b, s // NX, s % NX] = jnp.dot(
                selt[s], rows, preferred_element_type=F32
            ).astype(BF16)

    def rs_msg(b, k, half, s):
        i = 0 if s > 0 else 1
        o = half * 64
        whole = pl.ds(o, 64)
        part = pl.ds(o + 32 * i, 32)
        if k == 1:
            src = ag.at[b, wx(y + 2), :, part] if half == 0 else ag.at[b, :, wx(x + 2), part]
            dst = rs1
        else:
            src = ag.at[b, wx(y + s), :, whole] if half == 0 else ag.at[b, :, wx(x + s), whole]
            dst = rs2
        j = (k - 1) * 4 + half * 2 + i
        return rcopy(
            src, dst.at[b, half, i], rs_s.at[b, j], rs_r.at[b, j], to_y(s) if half == 0 else to_x(s)
        )

    def last_msg(b, half, j):
        whole = pl.ds(half * 64, 64)
        s = HOPS[j]
        src = ag.at[b, y, wx(x + s), whole] if half == 0 else ag.at[b, wx(y + s), x, whole]
        k = 8 + half * 3 + j
        return rcopy(
            src, rs3.at[b, half, j], rs_s.at[b, k], rs_r.at[b, k], to_x(s) if half == 0 else to_y(s)
        )

    def rs_step(k, b):
        for half in (0, 1):
            o = half * 64
            whole = pl.ds(o, 64)
            if k == 1:
                for s in (1, -1):
                    rs_msg(b, 1, half, s).start()
            elif k == 2:
                for i, s in ((0, 1), (1, -1)):
                    rs_msg(b, 1, half, s).wait_recv()
                    part = pl.ds(o + 32 * i, 32)

                    def add(j, carry):
                        yy, xx = (wx(y + s), j) if half == 0 else (j, wx(x + s))
                        ag[b, yy, xx, part] = (
                            ag[b, yy, xx, part].astype(F32) + rs1[b, half, i, j].astype(F32)
                        ).astype(BF16)
                        return carry

                    lax.fori_loop(0, 4, add, 0)
                    rs_msg(b, 2, half, s).start()
            elif k == 3:
                for s in (1, -1):
                    rs_msg(b, 2, half, s).wait_recv()

                def merge(j, carry):
                    yy, xx = (y, j) if half == 0 else (j, x)
                    ag[b, yy, xx, whole] = (
                        ag[b, yy, xx, whole].astype(F32)
                        + rs2[b, half, 0, j].astype(F32)
                        + rs2[b, half, 1, j].astype(F32)
                    ).astype(BF16)
                    return carry

                lax.fori_loop(0, 4, merge, 0)
                for j in range(3):
                    last_msg(b, half, j).start()
            elif k == 4:
                total = ag[b, y, x, whole].astype(F32)
                for j in range(3):
                    last_msg(b, half, j).wait_recv()
                    total = total + rs3[b, half, j].astype(F32)
                rigv[b, whole] = total.astype(BF16)
        if k == 4:
            out_copy(0, b).start()

    own_copy(0).wait()
    near(0, "start")
    for k in range(3):
        mt_msg(k).start()
    for n in range(1, NQ):
        own_copy(n).wait()
    near(1, "start")
    for k in range(3):
        mt_msg(k).wait_recv()
    for k in range(3, 6):
        mt_msg(k).start()
    near(0, "wait_recv")
    ag_own(0)
    near_done(1)
    ag_own(1)
    for k in range(3, 6):
        mt_msg(k).wait_recv()
    mt_msg(6).start()
    build_slots(0)
    core_copy.wait()
    ag_on(0)
    ag_own(2)
    for n in range(NQ, 2 * NQ):
        own_copy(n).wait()
    near(2, "start")

    def h_tick(n, carry):
        ag_on(n)
        when(n == 2, lambda: near_done(2))
        ag_own(n + 2)
        when(n == 1, lambda: near_on(2))
        ag_done(n - 1)
        compute_h(n - 1)
        return carry

    lax.fori_loop(1, NQ + 1, h_tick, 0)
    mt_msg(6).wait_recv()
    build_slots(1)
    build_gates()
    d2_msg(NQ - 1).wait_recv()
    turn(NQ - 1, 1)

    def sent(n, carry):
        for kind in range(2):
            for half, s in SIDES:
                ag_msg(n, kind, half, s).wait_send()
        d2_msg(n).wait_send()
        return carry

    steps = {
        "o": ag_on,
        "u": compute_upper,
        "c": gather_r,
        "k": lambda q: lower_r(q, 0),
        "l": lambda q: lower_r(q, 1),
        "t": form_term,
        "b": lambda b: form_back(b, 1),
        "a": lambda b: form_back(b, 0),
        "s": scatter_b,
    }
    cleared = False
    for name, i in ORDER:
        if name == "b" and not cleared:
            lax.fori_loop(0, NQ, sent, 0)
            near(0, "wait_send")
            near(1, "wait_send")
            cleared = True
        if name[0] == "z":
            z_step(int(name[1]), i)
        elif name[0] == "r":
            rs_step(int(name[1]), i)
        else:
            steps[name](i)
        if name == "o" and i == NQ + 1:
            ag_own(2 * NQ - 1)
    lax.fori_loop(NQ, 2 * NQ, sent, 0)
    near(2, "wait_send")

    for k in range(7):
        mt_msg(k).wait_send()

    def flushed(q, carry):
        d2_back(q).wait_send()
        for k in range(1, 5):
            for s in (1, -1):
                z_msg(q, k, s).wait_send()
        for half, s in SIDES:
            for k in (1, 2):
                rs_msg(q, k, half, s).wait_send()
        for half in (0, 1):
            for j in range(3):
                last_msg(q, half, j).wait_send()
        return carry

    lax.fori_loop(0, NQ, flushed, 0)
    for which in (0, 1):
        for i in range(NQ):
            out_copy(which, i).wait()


def finish(rig_ref, cg_ref, rig_out, cg_out):
    rig_out[...] = rig_ref[...]
    for e in (0, 1):
        cg_out[:, e, :] = cg_ref[e]


def local(hidden_in, rank_grad, gates, expert_ids, cores):
    vmem = pl.BlockSpec(memory_space=pltpu.VMEM)
    hbm = pl.BlockSpec(memory_space=pl.ANY)
    dma = pltpu.SemaphoreType.DMA
    rig, cg = pl.pallas_call(
        body,
        out_shape=(
            jax.ShapeDtypeStruct((TOK, NQ * CQ), BF16),
            jax.ShapeDtypeStruct((2, TOK, NQ * CQ), F32),
        ),
        in_specs=[hbm, hbm, vmem, vmem, hbm],
        out_specs=(hbm, hbm),
        scratch_shapes=[
            pltpu.VMEM((2 * NQ, NY, NX, TOK, CQ), BF16),
            pltpu.VMEM((2, NY, NX, 16, TOK), BF16),
            pltpu.VMEM((2, NQ * CQ, NQ * CQ), BF16),
            pltpu.VMEM((2 * NQ, 2, 2, NS, CAP, CQ), BF16),
            pltpu.VMEM((2 * NQ, 2, NS, CAP, CQ), BF16),
            pltpu.VMEM((NQ, 2, 2 * ROWS, CQ), F32),
            pltpu.VMEM((NQ, 2, 2 * ROWS, CQ), BF16),
            pltpu.VMEM((2, NQ * CQ, 2 * ROWS), BF16),
            pltpu.VMEM((NQ, 4, NS, CAP, CQ), BF16),
            pltpu.VMEM((NS, 4 * CAP, TOK), BF16),
            pltpu.VMEM((NS, TOK, 4 * CAP), BF16),
            pltpu.VMEM((2, 2, ROWS, TOK), F32),
            pltpu.VMEM((2 * NS * 8, TOK), F32),
            pltpu.VMEM((2 * NS * 8, TOK), F32),
            pltpu.VMEM((2 * NS * 8, TOK), F32),
            pltpu.VMEM((NQ, 2, TOK, CQ), BF16),
            pltpu.VMEM((NQ, 2, TOK, CQ), BF16),
            pltpu.VMEM((NQ, 2, 2, TOK, CQ), BF16),
            pltpu.VMEM((NQ, 2, 2, TOK, CQ), BF16),
            pltpu.VMEM((NQ, 2, 2, TOK, CQ), BF16),
            pltpu.VMEM((NQ, 2, 2, TOK, CQ), BF16),
            pltpu.VMEM((NQ, 2, 2, 4, 32, CQ), BF16),
            pltpu.VMEM((NQ, 2, 2, 4, 64, CQ), BF16),
            pltpu.VMEM((NQ, 2, 3, 64, CQ), BF16),
            pltpu.VMEM((NQ, TOK, CQ), BF16),
            pltpu.VMEM((NQ, 2, TOK, CQ), F32),
            dma((2 * NQ,)), dma((2, NQ)),
            dma, dma((3, 8)), dma((3, 8)), dma((2 * NQ, 8)), dma((2 * NQ, 8)), dma((7,)), dma((7,)),
            dma((3 * NQ,)), dma((3 * NQ,)), dma((NQ, 8)), dma((NQ, 8)),
            dma((NQ, 14)), dma((NQ, 14)),
        ],
        compiler_params=pltpu.CompilerParams(
            collective_id=0, has_side_effects=True, vmem_limit_bytes=62 * 1024 * 1024
        ),
        cost_estimate=pl.CostEstimate(
            flops=14_000_000_000, bytes_accessed=8_000_000, transcendentals=2_000_000
        ),
        name="moe_core_backward",
    )(hidden_in, rank_grad, expert_ids.T, gates.T, cores)
    part = TOK // 1
    return pl.pallas_call(
        finish,
        grid=(1,),
        out_shape=(
            jax.ShapeDtypeStruct((TOK, NQ * CQ), BF16),
            jax.ShapeDtypeStruct((TOK, 2, NQ * CQ), F32),
        ),
        in_specs=[
            pl.BlockSpec((part, NQ * CQ), lambda i: (i, 0)),
            pl.BlockSpec((2, part, NQ * CQ), lambda i: (0, i, 0)),
        ],
        out_specs=(
            pl.BlockSpec((part, NQ * CQ), lambda i: (i, 0)),
            pl.BlockSpec((part, 2, NQ * CQ), lambda i: (i, 0, 0)),
        ),
        compiler_params=pltpu.CompilerParams(vmem_limit_bytes=16 * 1024 * 1024),
        name="place_outputs",
    )(rig, cg)


def solution(mesh):
    in_specs = (
        P(("dp", "expert"), None),
        P(("dp", "expert"), None),
        P(("dp", "expert"), None),
        P(("dp", "expert"), None),
        P("expert", None, None),
    )
    out_specs = (P(("dp", "expert"), None), P("dp", "expert", None))
    return jax.shard_map(local, mesh=mesh, in_specs=in_specs, out_specs=out_specs, check_vma=False)
```
